256 devices in a mesh: loop: 32 (over y_lo, z, core), grp: 8 (over y_hi, x).
Axes of the slice: x: 4, y: 4 (y_hi: 2, y_lo: 2; y = y_hi * 2 + y_lo), z: 8, core: 2. Of those that a mesh axis runs over, the one named last changes fastest.
Arguments:
- query: float32 [16384, 1024], P(('loop', 'grp')), may hold values from -5 to 5
- document: float32 [16384, 1024], P(('loop', 'grp')), may hold values from -5 to 5
- pair_index: int32 [16384], P(('loop', 'grp')), may hold values from 0 to 16383, each once
Outputs:
- row_loss: float32 [16384], P(('loop', 'grp'))
- col_loss: float32 [16384], P(('loop', 'grp'))
- grad_query: float32 [16384, 1024], P(('loop', 'grp'))
- grad_doc: float32 [16384, 1024], P(('loop', 'grp'))
The draws below stay inside these ranges and needn't reach their ends.
Inputs may be any that keep to these rules, and one draw needn't show every extreme that they name: `pair_index`: a permutation of 0 to 16383.
All inputs are finite; a program needn't handle non-finite values.
Results may differ from the reference program's by a relative error of at most 0.0003.
Values sent between devices are 32-bit elements; how exact they have to be, the bound alone decides.
No kernel may reach another device: no remote copies, remote signals or barrier semaphores. Data moves between devices by JAX's collectives and lax.ppermute only.
A program may use at most 64 MiB of HBM per device.

```python
import math
import jax
import jax.numpy as jnp
from jax import lax

D = 1024
ROWS = 16384


def embed_pair(key, lowest):
    keys = jax.random.split(key, 10)
    shape = (ROWS, D)

    def base_rows(key_normal, key_uniform, key_scale, common):
        gauss = jax.random.truncated_normal(key_normal, -4.0, 4.0, shape, jnp.float32)
        mixed = gauss
        scale = jnp.exp(jax.random.uniform(key_scale, (ROWS,), jnp.float32, math.log(lowest), math.log(4.0)))
        return mixed * scale[:, None] / 32.0
    common = jax.random.truncated_normal(keys[0], -3.0, 3.0, (D,), jnp.float32)
    document = base_rows(keys[1], keys[2], keys[3], common)
    query = base_rows(keys[4], keys[5], keys[6], common)
    index = jnp.arange(ROWS, dtype=jnp.int32)
    root = math.sqrt(D)
    strength = jnp.exp(jax.random.uniform(keys[7], (ROWS,), jnp.float32, math.log(8.0), math.log(14.0)))
    fresh = jax.random.uniform(keys[8], shape, jnp.float32, -1.7, 1.7) / root
    noise = jax.random.truncated_normal(keys[9], -4.0, 4.0, shape, jnp.float32)
    twin = (1.0 - 0.1 / jnp.roll(strength, 323))[:, None] * jnp.roll(fresh, 1, axis=0) + 0.02 * noise / root
    document = jnp.where((index % 64 == 7)[:, None], fresh, document)
    document = jnp.where((index % 64 == 8)[:, None], twin, document)
    aligned = strength[:, None] * jnp.roll(document, -322, axis=0)
    query = jnp.where((index % 64 == 5)[:, None], aligned, query)
    return (query, document)


def draw_query(key, part):
    query, document = embed_pair(key, 0.4)
    return query


def draw_document(key, part):
    query, document = embed_pair(key, 0.4)
    return document


def setup_inputs(seed: int = 0) -> dict:
    splits = jax.random.split(jax.random.key(seed), 4)
    return {
        "query": draw_query(jax.random.fold_in(splits[3], 71), 0),
        "document": draw_document(jax.random.fold_in(splits[3], 71), 0),
        "pair_index": jax.random.permutation(splits[2], ROWS).astype(jnp.int32),
    }


inv_temp = 20.0


def reference(query, document, pair_index):
    row_count = query.shape[0]
    width = query.shape[1]
    block = math.gcd(row_count, 512)
    block_count = row_count // block
    query_blocks = query.reshape(block_count, block, width)
    pair_blocks = pair_index.reshape(block_count, block)
    column_ids = jnp.arange(row_count, dtype=jnp.int32)

    def score_block(query_block):
        return jnp.dot(query_block, document.T, precision=lax.Precision.HIGHEST, preferred_element_type=jnp.float32) * inv_temp

    def first_sweep(carry, inputs):
        col_top, col_sum, col_pos = carry
        query_block, pair_block = inputs
        scores = score_block(query_block)
        matches = (pair_block[:, None] == column_ids[None, :]).astype(jnp.float32)
        row_top = jnp.max(scores, axis=1)
        row_lse = row_top + jnp.log(jnp.sum(jnp.exp(scores - row_top[:, None]), axis=1))
        row_pos = jnp.sum(matches * scores, axis=1)
        new_top = jnp.maximum(col_top, jnp.max(scores, axis=0))
        col_sum = col_sum * jnp.exp(col_top - new_top) + jnp.sum(jnp.exp(scores - new_top[None, :]), axis=0)
        col_pos = col_pos + jnp.sum(matches * scores, axis=0)
        return (new_top, col_sum, col_pos), (row_lse, row_pos)

    start = (jnp.full((row_count,), -1e30, jnp.float32), jnp.zeros((row_count,), jnp.float32), jnp.zeros((row_count,), jnp.float32))
    (col_top, col_sum, col_pos), (row_lse, row_pos) = lax.scan(first_sweep, start, (query_blocks, pair_blocks))
    col_lse = col_top + jnp.log(col_sum)

    def second_sweep(grad_doc, inputs):
        query_block, pair_block, lse_block = inputs
        scores = score_block(query_block)
        matches = (pair_block[:, None] == column_ids[None, :]).astype(jnp.float32)
        weights = (jnp.exp(scores - lse_block[:, None]) + jnp.exp(scores - col_lse[None, :]) - 2.0 * matches) * 0.5
        grad_block = jnp.dot(weights, document, precision=lax.Precision.HIGHEST, preferred_element_type=jnp.float32) * inv_temp
        grad_doc = grad_doc + jnp.dot(weights.T, query_block, precision=lax.Precision.HIGHEST, preferred_element_type=jnp.float32) * inv_temp
        return grad_doc, grad_block

    grad_doc, grad_blocks = lax.scan(second_sweep, jnp.zeros((row_count, width), jnp.float32), (query_blocks, pair_blocks, row_lse))
    row_loss = (row_lse - row_pos).reshape(row_count)
    col_loss = col_lse - col_pos
    return row_loss, col_loss, grad_blocks.reshape(row_count, width), grad_doc
```

```python
import functools

import jax
import jax.numpy as jnp
from jax import lax
from jax.experimental import pallas as pl
from jax.experimental.pallas import tpu as pltpu
from jax.sharding import PartitionSpec as P

inv_temp = 20.0
f32, bf16 = jnp.float32, jnp.bfloat16
AXES = ("loop", "grp")
OWN = 64
CHIP = 2 * OWN
WIDE = 1024
BLOCK = 256
VMEM_LIMIT = 60 * 1024 * 1024


def flat(x, y, z, c):
    return (((y % 2) * 8 + z) * 2 + c) * 8 + (y // 2) * 4 + x


def permutation(move):
    return [
        (flat(x, y, z, c), flat(*move(x, y, z, c)))
        for x in range(4)
        for y in range(4)
        for z in range(8)
        for c in range(2)
    ]


def along_first(delta):
    return permutation(
        lambda x, y, z, c: ((x + delta) % 4, y, z, c) if c == 0 else (x, (y + delta) % 4, z, c)
    )


def along_second(delta):
    return permutation(
        lambda x, y, z, c: (x, (y + delta) % 4, z, c) if c == 0 else ((x + delta) % 4, y, z, c)
    )


def along_z(delta):
    return permutation(
        lambda x, y, z, c: (x, y, (z + delta) % 8, c) if c == 0 else (x, y, (z - delta) % 8, c)
    )


SWAP = permutation(lambda x, y, z, c: (x, y, z, 1 - c))


def send(value, perm):
    return lax.ppermute(value, AXES, perm)


def split(value):
    high = value.astype(bf16)
    return high, (value - high.astype(f32)).astype(bf16)


def dot3(ah, al, bh, bl, dims):
    dot = functools.partial(
        lax.dot_general, dimension_numbers=(dims, ((), ())), preferred_element_type=f32
    )
    return dot(ah, bh) + dot(ah, bl) + dot(al, bh)


def whole(count):
    return [pl.BlockSpec(memory_space=pltpu.VMEM)] * count


def call(kernel, shapes, inputs, scratch=(), with_place=True):
    specs = whole(len(inputs))
    if with_place:
        specs = [pl.BlockSpec(memory_space=pltpu.SMEM)] + specs[1:]
    return pl.pallas_call(
        kernel,
        out_shape=[jax.ShapeDtypeStruct(s, t) for s, t in shapes],
        in_specs=specs,
        out_specs=whole(len(shapes)),
        scratch_shapes=list(scratch),
        compiler_params=pltpu.CompilerParams(vmem_limit_bytes=VMEM_LIMIT),
    )(*inputs)


def z_row(z, c, steps):
    sign = 1 - 2 * c
    return lax.rem(z + sign * steps + 8, 8) * CHIP


def doc_row(x, y, c, first, second):
    dx = jnp.where(c == 0, first, second)
    dy = jnp.where(c == 0, second, first)
    return (lax.rem(y + dy, 4) * 4 + lax.rem(x + dx, 4)) * OWN


def doc_ids(block, z, c):
    row = block * BLOCK + lax.broadcasted_iota(jnp.int32, (BLOCK, 1), 0)
    y, x, r = row // 256, (row // OWN) % 4, row % OWN
    return (flat(x, y, z, c) * OWN + r).astype(f32)


def score_kernel(place, *refs):
    v, own1, own2, own3, own4, oth1, oth2, oth3, oth4 = refs[:9]
    p1, r1, r3, r2t, r2b = refs[9:14]
    st, qh, ql, dh, dl, pair, row_stats, col_stats = refs[14:]
    x, y, z, c = place[0], place[1], place[2], place[3]

    def put(high, low, ref, start, count, row):
        h, l = split(ref[start : start + count, :])
        at = pl.ds(pl.multiple_of(row, 32), count)
        high[at, :] = h
        low[at, :] = l

    def put_block(ref, row, first, both=True):
        put(qh, ql, ref, 0, OWN, row + first * OWN)
        if both:
            put(qh, ql, ref, OWN + 8, OWN, row + (1 - first) * OWN)
        pair[:, pl.ds(pl.multiple_of(row, CHIP), CHIP)] = ref[OWN : OWN + 8, :CHIP]

    put_block(v, z_row(z, c, 0), c)
    for k, ref in enumerate((own1, own2, own3, own4)):
        put_block(ref, z_row(z, c, k + 1), c, k < 3)
    for k, ref in enumerate((oth1, oth2, oth3, oth4)):
        put_block(ref, z_row(z, c, -k - 1), 1 - c, k < 3)
    for a in range(4):
        put(dh, dl, p1, a * OWN, OWN, doc_row(x, y, c, a, 0))
        put(dh, dl, r1, a * OWN, OWN, doc_row(x, y, c, a, 1))
        put(dh, dl, r3, a * OWN, OWN, doc_row(x, y, c, a, 3))
        half = (r2t, r2b)[a // 2]
        put(dh, dl, half, a % 2 * OWN, OWN, doc_row(x, y, c, a, 2))

    pairs = pair[0:1, :]
    lane = lax.broadcasted_iota(jnp.int32, (BLOCK, 128), 1)
    for b in range(WIDE // BLOCK):
        at = slice(b * BLOCK, (b + 1) * BLOCK)
        s = dot3(dh[at, :], dl[at, :], qh[...], ql[...], ((1,), (1,))) * inv_temp
        st[at, :] = s
        picked = jnp.where(pairs == doc_ids(b, z, c), s, 0.0)
        cm = jnp.max(s, axis=1, keepdims=True)
        ce = jnp.sum(jnp.exp(s - cm), axis=1, keepdims=True)
        cp = jnp.sum(picked, axis=1, keepdims=True)
        mixed = jnp.where(lane == 0, cm, jnp.where(lane == 1, ce, cp))
        col_stats[:, at] = mixed.T[0:8, :]
        bm = jnp.max(s, axis=0, keepdims=True)
        bp = jnp.sum(picked, axis=0, keepdims=True)
        if b == 0:
            rm, rp = bm, bp
            re = jnp.sum(jnp.exp(s - rm), axis=0, keepdims=True)
        else:
            top = jnp.maximum(rm, bm)
            re = re * jnp.exp(rm - top) + jnp.sum(jnp.exp(s - top), axis=0, keepdims=True)
            rm, rp = top, rp + bp
    row_stats[...] = jnp.concatenate([rm, re, rp, jnp.zeros((5, WIDE), f32)], axis=0)


def combine_kernel(a, b, d, e, ab, de):
    for left, right, out in ((a, b, ab), (d, e, de)):
        lm, rm = left[0:1, :], right[0:1, :]
        top = jnp.maximum(lm, rm)
        total = left[1:2, :] * jnp.exp(lm - top) + right[1:2, :] * jnp.exp(rm - top)
        out[...] = jnp.concatenate(
            [top, total, left[2:3, :] + right[2:3, :], jnp.zeros((5, WIDE), f32)], axis=0
        )


def doc_grad_kernel(place, st, qh, ql, pair, row_stats, col_stats, *refs):
    g0, g1, g2t, g2b, g3, wh, wl, losses, full = refs
    x, y, z, c = place[0], place[1], place[2], place[3]
    row_lse = row_stats[0:1, :] + jnp.log(row_stats[1:2, :])
    col_lse = col_stats[0:1, :] + jnp.log(col_stats[1:2, :])
    losses[...] = jnp.concatenate(
        [row_lse - row_stats[2:3, :], col_lse - col_stats[2:3, :], jnp.zeros((6, WIDE), f32)],
        axis=0,
    )
    pairs = pair[0:1, :]
    for b in range(WIDE // BLOCK):
        at = slice(b * BLOCK, (b + 1) * BLOCK)
        s = st[at, :]
        cl = jnp.broadcast_to(col_lse[:, at], (128, BLOCK)).T[:, 0:1]
        w = (jnp.exp(s - row_lse) + jnp.exp(s - cl)) * (0.5 * inv_temp)
        w = w - jnp.where(pairs == doc_ids(b, z, c), inv_temp, 0.0)
        h, l = split(w)
        wh[at, :] = h
        wl[at, :] = l
        full[at, :] = dot3(h, l, qh[...], ql[...], ((1,), (0,)))

    def take(a, second):
        return full[pl.ds(pl.multiple_of(doc_row(x, y, c, a, second), OWN), OWN), :]

    for a in range(4):
        at = slice(a * OWN, (a + 1) * OWN)
        g0[at, :] = take(a, 0)
        g1[at, :] = take(a, 1)
        g3[at, :] = take(a, 3)
        (g2t, g2b)[a // 2][a % 2 * OWN : (a % 2 + 1) * OWN, :] = take(a, 2)


def query_grad_kernel(place, wh, wl, dh, dl, *refs):
    p4, p3, p2, p1, p0, first, second, full = refs
    z, c = place[2], place[3]
    for b in range(WIDE // BLOCK):
        at = slice(b * BLOCK, (b + 1) * BLOCK)
        full[at, :] = dot3(wh[:, at], wl[:, at], dh[...], dl[...], ((0,), (0,)))

    def copy(out, start, row, core):
        at = pl.ds(pl.multiple_of(row + core * OWN, OWN), OWN)
        out[start : start + OWN, :] = full[at, :]

    copy(p4, 0, z_row(z, c, 4), c)
    for k, out in ((3, p3), (2, p2), (1, p1)):
        copy(out, 0, z_row(z, c, k), c)
        copy(out, OWN, z_row(z, c, k), 1 - c)
    copy(p0, 0, z_row(z, c, 0), c)
    copy(first, 0, z_row(z, c, 4), 1 - c)
    for k, out, start in ((3, first, OWN), (2, second, 0), (1, second, CHIP)):
        copy(out, start, z_row(z, c, -k), 1 - c)
        copy(out, start + OWN, z_row(z, c, -k), c)
    copy(second, 2 * CHIP, z_row(z, c, 0), 1 - c)


def body(query, document, pair_index):
    loop, grp = lax.axis_index("loop"), lax.axis_index("grp")
    c, z = loop % 2, (loop // 2) % 8
    x, y = grp % 4, (grp // 4) * 2 + loop // 16
    place = jnp.stack([x, y, z, c]).astype(jnp.int32)
    with jax.named_scope("gather"):
        pairs = jnp.concatenate([pair_index, pair_index]).astype(f32)
        mine = jnp.arange(CHIP, dtype=jnp.int32) // OWN == c
        pairs = jnp.pad(jnp.where(mine, pairs, 0.0)[None, :], ((0, 7), (0, WIDE - CHIP)))
        other = send(jnp.concatenate([query, pairs]), SWAP)
        v = jnp.concatenate([query, pairs + other[OWN:], other[:OWN]])
        own1 = send(v, along_z(-1))
        a1, a3 = send(document, along_first(-1)), send(document, along_first(1))
        own2 = send(own1, along_z(-1))
        a2t, a2b = send(a1[:32], along_first(-1)), send(a3[32:], along_first(1))
        p1 = jnp.concatenate([document, a1, a2t, a2b, a3])
        r1, r3 = send(p1, along_second(-1)), send(p1, along_second(1))
        own3 = send(own2, along_z(-1))
        own4 = send(own3[: OWN + 8], along_z(-1))
        r2t, r2b = send(r1[:CHIP], along_second(-1)), send(r3[CHIP:], along_second(1))
        own = [own1, own2, own3, own4]
        oth = [send(piece, SWAP) for piece in own]
    square = (WIDE, WIDE)
    st, qh, ql, dh, dl, pair, rows, cols = call(
        score_kernel,
        [(square, f32)] + [(square, bf16)] * 4 + [((8, WIDE), f32)] * 3,
        [place, v, *own, *oth, p1, r1, r3, r2t, r2b],
    )
    with jax.named_scope("totals"):
        for row_move, col_move in (
            (lambda x, y, z, c: (x, y, z, 1 - c), lambda x, y, z, c: (x ^ 1, y, z, c)),
            (lambda x, y, z, c: (x, y, z ^ 1, c), lambda x, y, z, c: (x ^ 2, y, z, c)),
            (lambda x, y, z, c: (x, y, z ^ 2, c), lambda x, y, z, c: (x, y ^ 1, z, c)),
            (lambda x, y, z, c: (x, y, z ^ 4, c), lambda x, y, z, c: (x, y ^ 2, z, c)),
        ):
            more_rows = send(rows, permutation(row_move))
            more_cols = send(cols, permutation(col_move))
            rows, cols = call(
                combine_kernel,
                [((8, WIDE), f32)] * 2,
                [rows, more_rows, cols, more_cols],
                with_place=False,
            )
    g0, g1, g2t, g2b, g3, wh, wl, losses = call(
        doc_grad_kernel,
        [((BLOCK, WIDE), f32)] * 2
        + [((CHIP, WIDE), f32)] * 2
        + [((BLOCK, WIDE), f32)]
        + [(square, bf16)] * 2
        + [((8, WIDE), f32)],
        [place, st, qh, ql, pair, rows, cols],
        [pltpu.VMEM(square, f32)],
    )
    q4, q3, q2, q1, q0, first, second = call(
        query_grad_kernel,
        [((n, WIDE), f32) for n in (OWN, CHIP, CHIP, CHIP, OWN, 3 * OWN, 5 * OWN)],
        [place, wh, wl, dh, dl],
        [pltpu.VMEM(square, f32)],
    )
    with jax.named_scope("scatter"):
        from1, from3 = send(g2t, along_second(1)), send(g2b, along_second(-1))
        g1 = jnp.concatenate([g1[:CHIP] + from1, g1[CHIP:]])
        g3 = jnp.concatenate([g3[:CHIP], g3[CHIP:] + from3])
        first, second = send(first, SWAP), send(second, SWAP)
        q4 = send(q4 + first[:OWN], along_z(1))
        q3 = q3 + first[OWN:]
        q3 = send(jnp.concatenate([q3[:OWN] + q4, q3[OWN:]]), along_z(1))
        g0 = g0 + send(g1, along_second(1)) + send(g3, along_second(-1))
        q2 = send(q2 + second[:CHIP] + q3, along_z(1))
        d0, d1, d2, d3 = (g0[k * OWN : (k + 1) * OWN] for k in range(4))
        from1, from3 = send(d2[:32], along_first(1)), send(d2[32:], along_first(-1))
        q1 = send(q1 + second[CHIP : 2 * CHIP] + q2, along_z(1))
        d1 = jnp.concatenate([d1[:32] + from1, d1[32:]])
        d3 = jnp.concatenate([d3[:32], d3[32:] + from3])
        grad_doc = d0 + send(d1, along_first(1)) + send(d3, along_first(-1))
        grad_query = q0 + second[2 * CHIP :] + q1[:OWN] + send(q1[OWN:], SWAP)
    row_loss = lax.dynamic_slice(losses[0], (z * CHIP + c * OWN,), (OWN,))
    col_loss = lax.dynamic_slice(losses[1], ((y * 4 + x) * OWN,), (OWN,))
    return row_loss, col_loss, grad_query, grad_doc


def solution(mesh):
    rows, flat_rows = P(AXES, None), P(AXES)
    return jax.shard_map(
        body,
        mesh=mesh,
        in_specs=(rows, rows, flat_rows),
        out_specs=(flat_rows, flat_rows, rows, rows),
        check_vma=False,
    )
```

```python
import functools

import jax
import jax.numpy as jnp
from jax import lax
from jax.experimental import pallas as pl
from jax.experimental.pallas import tpu as pltpu
from jax.sharding import PartitionSpec as P

inv_temp = 20.0
f32, bf16 = jnp.float32, jnp.bfloat16
AXES = ("loop", "grp")
OWN = 64
CHIP = 2 * OWN
PIECE = OWN + 8
WIDE = 1024
BLOCK = 256
EARLY_Q, EARLY_D = 640, 768
VMEM_LIMIT = 12 * 1024 * 1024
GROUPS = ((0, 0), (0, 2), (1, 0), (3, 2), (1, 2), (3, 0), (2, 0), (2, 2))


def flat(x, y, z, c):
    return (((y & 1) * 8 + z) * 2 + c) * 8 + (y >> 1) * 4 + x


def permutation(move):
    return [
        (flat(x, y, z, c), flat(*move(x, y, z, c)))
        for x in range(4)
        for y in range(4)
        for z in range(8)
        for c in range(2)
    ]


def along_first(delta):
    return permutation(
        lambda x, y, z, c: ((x + delta) % 4, y, z, c) if c == 0 else (x, (y + delta) % 4, z, c)
    )


def along_second(delta):
    return permutation(
        lambda x, y, z, c: (x, (y + delta) % 4, z, c) if c == 0 else ((x + delta) % 4, y, z, c)
    )


def along_z(delta):
    return permutation(
        lambda x, y, z, c: (x, y, (z + delta) % 8, c) if c == 0 else (x, y, (z - delta) % 8, c)
    )


SWAP = permutation(lambda x, y, z, c: (x, y, z, 1 - c))


def send(value, perm):
    return lax.ppermute(value, AXES, perm)


together = lax.optimization_barrier


def split(value):
    high = value.astype(bf16)
    return high, (value - high.astype(f32)).astype(bf16)


def dot3(ah, al, bh, bl, dims):
    dot = functools.partial(
        lax.dot_general, dimension_numbers=(dims, ((), ())), preferred_element_type=f32
    )
    return dot(ah, bh) + dot(ah, bl) + dot(al, bh)


def call(kernel, shapes, inputs, scratch=(), aliases=()):
    held = [pltpu.with_memory_space_constraint(a, pltpu.VMEM) for a in inputs[1:]]
    return pl.pallas_call(
        kernel,
        out_shape=[pltpu.VMEM(s, t) for s, t in shapes],
        in_specs=[pl.BlockSpec(memory_space=pltpu.SMEM)]
        + [pl.BlockSpec(memory_space=pltpu.VMEM)] * len(held),
        out_specs=[pl.BlockSpec(memory_space=pltpu.VMEM)] * len(shapes),
        scratch_shapes=list(scratch),
        input_output_aliases=dict(aliases),
        compiler_params=pltpu.CompilerParams(vmem_limit_bytes=VMEM_LIMIT),
    )(inputs[0], *held)


def block_z(z, c, block):
    sign = 1 - 2 * c
    steps = (0, 1, -1, 2, -2, 3, -3, 4)[block]
    return (z + sign * steps) & 7


def doc_chip(x, y, c, first, second):
    dx = jnp.where(c == 0, first, second)
    dy = jnp.where(c == 0, second, first)
    return ((y + dy) & 3) * 4 + ((x + dx) & 3)


def doc_piece(x, y, c, piece):
    second, first = GROUPS[piece // 2]
    return doc_chip(x, y, c, first + piece % 2, second)


def doc_ids(block, x, y, z, c):
    row = lax.broadcasted_iota(jnp.int32, (OWN, 1), 0)
    ids = []
    for piece in range(block * 4, block * 4 + 4):
        chip = doc_piece(x, y, c, piece)
        ids.append(row + flat(chip & 3, chip >> 2, z, c) * OWN)
    return jnp.concatenate(ids, axis=0).astype(f32)


def put(high, low, ref, start, count, row):
    h, l = split(ref[start : start + count, :])
    high[row : row + count, :] = h
    low[row : row + count, :] = l


def pack_kernel(place, query, pairs, out):
    out[0:OWN, :] = query[...]
    out[OWN:, :] = jnp.zeros((8, WIDE), f32)
    out[OWN : OWN + 1, :OWN] = pairs[...]


def stack_kernel(place, *refs):
    for k, ref in enumerate(refs[:-1]):
        refs[-1][k * PIECE : (k + 1) * PIECE, :] = ref[...]


def put_queries(qh, ql, pair, block, mine, mine_at, other, other_at):
    put(qh, ql, mine, mine_at, OWN, block * CHIP)
    put(qh, ql, other, other_at, OWN, block * CHIP + OWN)
    first = mine[mine_at + OWN : mine_at + PIECE, :CHIP]
    last = other[other_at + OWN : other_at + PIECE, :CHIP]
    pair[:, block * CHIP : (block + 1) * CHIP] = first + pltpu.roll(last, OWN, 1)


def early_kernel(place, u, uo, a1, b1, a2, b2, s12, p1t, p1b, r1t, r1b, r3t, r3b, *outs):
    st, qh, ql, dh, dl, pair = outs
    put_queries(qh, ql, pair, 0, u, 0, uo, 0)
    put_queries(qh, ql, pair, 1, a1, 0, b1, 0)
    put_queries(qh, ql, pair, 2, s12, PIECE, s12, 0)
    put_queries(qh, ql, pair, 3, a2, 0, b2, 0)
    put_queries(qh, ql, pair, 4, s12, 3 * PIECE, s12, 2 * PIECE)
    for k, ref in enumerate((p1t, p1b, r1t, r3b, r1b, r3t)):
        put(dh, dl, ref, 0, CHIP, k * CHIP)
    q = slice(0, EARLY_Q)
    for b in range(3):
        at = slice(b * BLOCK, (b + 1) * BLOCK)
        s = dot3(dh[at, :], dl[at, :], qh[q, :], ql[q, :], ((1,), (1,)))
        st[at, q] = s * inv_temp


def score_kernel(place, a3, b3, a4, s34, r2t, r2b, *refs):
    st, qh, ql, dh, dl, pair, keep, give, mixed = refs[6:]
    x, y, z, c = place[0], place[1], place[2], place[3]
    put_queries(qh, ql, pair, 5, a3, 0, b3, 0)
    put_queries(qh, ql, pair, 6, s34, PIECE, s34, 0)
    put_queries(qh, ql, pair, 7, a4, 0, s34, 2 * PIECE)
    put(dh, dl, r2t, 0, CHIP, EARLY_D)
    put(dh, dl, r2b, 0, CHIP, EARLY_D + CHIP)
    pairs = pair[0:1, :]
    lane = lax.broadcasted_iota(jnp.int32, (BLOCK, 128), 1)
    for b in range(4):
        at = slice(b * BLOCK, (b + 1) * BLOCK)
        q = slice(EARLY_Q if b < 3 else 0, WIDE)
        s = dot3(dh[at, :], dl[at, :], qh[q, :], ql[q, :], ((1,), (1,)))
        st[at, q] = s * inv_temp
        s = st[at, :]
        picked = jnp.where(pairs == doc_ids(b, x, y, z, c), s, 0.0)
        cm = jnp.max(s, axis=1, keepdims=True)
        ce = jnp.sum(jnp.exp(s - cm), axis=1, keepdims=True)
        cp = jnp.sum(picked, axis=1, keepdims=True)
        stats = jnp.where(lane == 0, cm, jnp.where(lane == 1, ce, cp))
        for a in range(4):
            row = pl.multiple_of(doc_piece(x, y, c, b * 4 + a) * OWN, OWN)
            mixed[pl.ds(row, OWN), :] = stats[a * OWN : (a + 1) * OWN, :]
        bm = jnp.max(s, axis=0, keepdims=True)
        bp = jnp.sum(picked, axis=0, keepdims=True)
        if b == 0:
            rm, rp = bm, bp
            re = jnp.sum(jnp.exp(s - rm), axis=0, keepdims=True)
        else:
            top = jnp.maximum(rm, bm)
            re = re * jnp.exp(rm - top) + jnp.sum(jnp.exp(s - top), axis=0, keepdims=True)
            rm, rp = top, rp + bp
    rows = jnp.concatenate([rm, re, rp, jnp.zeros((5, WIDE), f32)], axis=0)

    def put_stats(row_out, col_out):
        for block in range(8):
            part = rows[:, block * CHIP : (block + 1) * CHIP]
            part = jnp.where(c == 0, part, pltpu.roll(part, OWN, 1))
            at = pl.multiple_of(block_z(z, c, block) * CHIP, CHIP)
            row_out[:, pl.ds(at, CHIP)] = part
        for b in range(4):
            at = slice(b * BLOCK, (b + 1) * BLOCK)
            col_out[:, at] = mixed[at, :].T[0:8, :]

    @pl.when(c == 0)
    def _():
        put_stats(keep, give)

    @pl.when(c == 1)
    def _():
        put_stats(give, keep)


def combine(a, b):
    top = jnp.maximum(a[0:1, :], b[0:1, :])
    total = a[1:2, :] * jnp.exp(a[0:1, :] - top) + b[1:2, :] * jnp.exp(b[0:1, :] - top)
    return jnp.concatenate(
        [top, total, a[2:3, :] + b[2:3, :], jnp.zeros((5, WIDE), f32)], axis=0
    )


def merge_kernel(place, keep, got, state):
    mine, theirs = keep[...], got[...]
    both = combine(mine, theirs)
    state[0:8, :] = jnp.where(place[3] == 0, both, mine)
    state[8:16, :] = jnp.where(place[3] == 0, both, theirs)


def round_kernel(place, state, got, out):
    out[0:8, :] = combine(state[0:8, :], got[0:8, :])
    out[8:16, :] = combine(state[8:16, :], got[8:16, :])


def last_round_kernel(place, state, got, mine, give):
    for out, at in ((mine, slice(0, 8)), (give, slice(8, 16))):
        so_far = state[at, :]
        out[...] = jnp.where(place[3] == 0, so_far, combine(so_far, got[at, :]))


def sum_kernel(place, *refs):
    *parts, out = refs
    out[...] = sum((part[...] for part in parts[1:]), parts[0][...])


def query_products(wh, wl, dh, dl, lo, hi):
    return dot3(wh[:, lo:hi], wl[:, lo:hi], dh[...], dl[...], ((0,), (0,)))


def weight_kernel(place, st, pair, mine, got, dh, dl, *refs):
    wh, wl, a4, a3, b3, first, losses, lse, columns = refs
    x, y, z, c = place[0], place[1], place[2], place[3]
    row_stats = jnp.where(c == 0, mine[...], got[...])
    col_stats = jnp.where(c == 0, got[...], mine[...])
    row_lse = row_stats[0:1, :] + jnp.log(row_stats[1:2, :])
    col_lse = col_stats[0:1, :] + jnp.log(col_stats[1:2, :])
    losses[...] = jnp.concatenate(
        [row_lse - row_stats[2:3, :], col_lse - col_stats[2:3, :], jnp.zeros((6, WIDE), f32)],
        axis=0,
    )
    lse[...] = jnp.broadcast_to(row_lse, (8, WIDE))
    parts = []
    for block in range(8):
        at = pl.multiple_of(block_z(z, c, block) * CHIP, CHIP)
        part = lse[:, pl.ds(at, CHIP)]
        parts.append(jnp.where(c == 0, part, pltpu.roll(part, OWN, 1)))
    row_lse = jnp.concatenate(parts, axis=1)[0:1, :]
    for b in range(4):
        at = slice(b * BLOCK, (b + 1) * BLOCK)
        columns[at, :] = jnp.broadcast_to(col_lse[:, at], (128, BLOCK)).T
    pairs = pair[0:1, :]
    for b in range(4):
        at = slice(b * BLOCK, (b + 1) * BLOCK)
        s = st[at, :]
        parts = []
        for a in range(4):
            row = pl.multiple_of(doc_piece(x, y, c, b * 4 + a) * OWN, OWN)
            parts.append(columns[pl.ds(row, OWN), :])
        cl = jnp.concatenate(parts, axis=0)[:, 0:1]
        w = (jnp.exp(s - row_lse) + jnp.exp(s - cl)) * (0.5 * inv_temp)
        w = w - jnp.where(pairs == doc_ids(b, x, y, z, c), inv_temp, 0.0)
        h, l = split(w)
        wh[at, :] = h
        wl[at, :] = l
    g = query_products(wh, wl, dh, dl, EARLY_Q, WIDE)
    a3[...] = g[:OWN]
    b3[...] = g[OWN:CHIP]
    a4[...] = g[2 * CHIP : 2 * CHIP + OWN]
    first[0:OWN, :] = g[2 * CHIP + OWN :]
    first[OWN : 2 * OWN, :] = g[CHIP + OWN : 2 * CHIP]
    first[2 * OWN :, :] = g[CHIP : CHIP + OWN]


def first_kernel(place, a4, b3, first, a4_out, b3_out):
    a4_out[...] = a4[...] + first[0:OWN, :]
    b3_out[...] = b3[...] + first[2 * OWN :, :]


def third_kernel(place, a3, first, from4, out):
    out[...] = a3[...] + first[OWN : 2 * OWN, :] + from4[...]


def query_kernel(place, wh, wl, dh, dl, a2, b2, a1, b1, near, second):
    g = query_products(wh, wl, dh, dl, 0, EARLY_Q)
    near[...] = g[:OWN]
    a1[...] = g[CHIP : CHIP + OWN]
    b1[...] = g[CHIP + OWN : 2 * CHIP]
    a2[...] = g[3 * CHIP : 3 * CHIP + OWN]
    b2[...] = g[3 * CHIP + OWN : 4 * CHIP]
    second[0:OWN, :] = g[4 * CHIP + OWN :]
    second[OWN : 2 * OWN, :] = g[4 * CHIP : 4 * CHIP + OWN]
    second[2 * OWN : 3 * OWN, :] = g[2 * CHIP + OWN : 3 * CHIP]
    second[3 * OWN : 4 * OWN, :] = g[2 * CHIP : 2 * CHIP + OWN]
    second[4 * OWN :, :] = g[OWN:CHIP]


def second_kernel(place, a2, b2, a1, b1, near, second, a2_out, b2_out, a1_out, b1_out, near_out):
    pairs = ((a2, a2_out), (b2, b2_out), (a1, a1_out), (b1, b1_out), (near, near_out))
    for k, (part, out) in enumerate(pairs):
        out[...] = part[...] + second[k * OWN : (k + 1) * OWN, :]


def doc_products(wh, wl, qh, ql, lo, hi):
    return dot3(wh[lo:hi, :], wl[lo:hi, :], qh[...], ql[...], ((1,), (0,)))


def far_doc_kernel(place, wh, wl, qh, ql, g1b, g3t, g2t, g2b):
    g = doc_products(wh, wl, qh, ql, 2 * BLOCK, WIDE)
    for k, out in enumerate((g1b, g3t, g2t, g2b)):
        out[...] = g[k * CHIP : (k + 1) * CHIP]


def side_doc_kernel(place, wh, wl, qh, ql, from1, from3, g1t, g3b):
    g = doc_products(wh, wl, qh, ql, BLOCK, 2 * BLOCK)
    g1t[...] = g[:CHIP] + from1[...]
    g3b[...] = g[CHIP:] + from3[...]


def near_doc_kernel(place, wh, wl, qh, ql, g0):
    g0[...] = doc_products(wh, wl, qh, ql, 0, BLOCK)


def fold_kernel(place, g0, y1t, y1b, y3t, y3b, d0, d1, d2, d3):
    for k, out in enumerate((d0, d1, d2, d3)):
        half = slice(k % 2 * OWN, (k % 2 + 1) * OWN)
        one, three = (y1t, y3t) if k < 2 else (y1b, y3b)
        out[...] = g0[k * OWN : (k + 1) * OWN, :] + one[half, :] + three[half, :]


def body(query, document, pair_index):
    loop, grp = lax.axis_index("loop"), lax.axis_index("grp")
    c, z = loop & 1, (loop >> 1) & 7
    x, y = grp & 3, (grp >> 2) * 2 + (loop >> 4)
    place = jnp.stack([x, y, z, c]).astype(jnp.int32)
    square = (WIDE, WIDE)
    piece, chip, block = (PIECE, WIDE), (CHIP, WIDE), (BLOCK, WIDE)
    own, totals = (OWN, WIDE), (8, WIDE)

    def one(kernel, shape, *inputs):
        return call(kernel, [(shape, f32)], [place, *inputs])[0]

    with jax.named_scope("gather"):
        d1, d3 = send(document, along_first(-1)), send(document, along_first(1))
        d2 = send(document, along_first(-2))
        u = one(pack_kernel, piece, query, pair_index.astype(f32)[None, :])
        uo = send(u, SWAP)
        a1 = send(u, along_z(-1))
        p1t = jnp.concatenate([document, d1])
        uo, p1t = together((uo, p1t))
        b1 = send(uo, along_z(-1))
        r1t, r3t = send(p1t, along_second(-1)), send(p1t, along_second(1))
        p1b = jnp.concatenate([d2, d3])
        a1, p1b = together((a1, p1b))
        a2 = send(a1, along_z(-1))
        r1b, r3b = send(p1b, along_second(-1)), send(p1b, along_second(1))
        b1, r1t, r3t = together((b1, r1t, r3t))
        b2 = send(b1, along_z(-1))
        r2t = send(r1t, along_second(-1))
        a2, r1b, r3b = together((a2, r1b, r3b))
        a3 = send(a2, along_z(-1))
        r2b = send(r3b, along_second(1))
        b3 = send(b2, along_z(-1))
        s12 = send(one(stack_kernel, (4 * PIECE, WIDE), a1, b1, a2, b2), SWAP)
        a3, r2t = together((a3, r2t))
        a4 = send(a3, along_z(-1))
        b3, r2b = together((b3, r2b))
        s34 = send(one(stack_kernel, (3 * PIECE, WIDE), a3, b3, a4), SWAP)
    tile = [(square, f32)] + [(square, bf16)] * 4 + [(totals, f32)]
    held = call(
        early_kernel,
        tile,
        [place, u, uo, a1, b1, a2, b2, s12, p1t, p1b, r1t, r1b, r3t, r3b],
    )
    st, qh, ql, dh, dl, pair, keep, give = call(
        score_kernel,
        tile + [(totals, f32)] * 2,
        [place, a3, b3, a4, s34, r2t, r2b, *held],
        [pltpu.VMEM((WIDE, 128), f32)],
        aliases=[(7 + k, k) for k in range(6)],
    )
    with jax.named_scope("totals"):
        state = one(merge_kernel, (16, WIDE), keep, send(give, SWAP))
        for move in (
            lambda x, y, z, c: (x, y, z ^ 1, c) if c == 0 else (x ^ 1, y, z, c),
            lambda x, y, z, c: (x, y, z ^ 2, c) if c == 0 else (x ^ 2, y, z, c),
            lambda x, y, z, c: (x, y, z ^ 4, c) if c == 0 else (x, y ^ 1, z, c),
        ):
            state = one(round_kernel, (16, WIDE), state, send(state, permutation(move)))
        last = [
            (source, target)
            for source, target in permutation(lambda x, y, z, c: (x, y ^ 2, z, c))
            if source // 8 % 2 == 1
        ]
        mine, give = call(
            last_round_kernel, [(totals, f32)] * 2, [place, state, send(state, last)]
        )
        got = send(give, SWAP)
    wh, wl, a4, a3, b3, first, losses = call(
        weight_kernel,
        [(square, bf16)] * 2 + [(own, f32)] * 3 + [((3 * OWN, WIDE), f32), (totals, f32)],
        [place, st, pair, mine, got, dh, dl],
        [pltpu.VMEM((8, WIDE), f32), pltpu.VMEM((WIDE, 128), f32)],
    )
    with jax.named_scope("scatter"):
        first = send(first, SWAP)
        g1b, g3t, g2t, g2b = call(far_doc_kernel, [(chip, f32)] * 4, [place, wh, wl, qh, ql])
        first, g1b, g3t, g2t, g2b, wh = together((first, g1b, g3t, g2t, g2b, wh))
        a4, b3 = call(first_kernel, [(own, f32)] * 2, [place, a4, b3, first])
        a4, b3, wh = together((a4, b3, wh))
        from1, from3 = send(g2t, along_second(1)), send(g2b, along_second(-1))
        a4, b3 = send(a4, along_z(1)), send(b3, along_z(1))
        y1b, y3t = send(g1b, along_second(1)), send(g3t, along_second(-1))
        a2, b2, a1, b1, near, second = call(
            query_kernel,
            [(own, f32)] * 5 + [((5 * OWN, WIDE), f32)],
            [place, wh, wl, dh, dl],
        )
        a4, b3, from1, from3, second, wh = together((a4, b3, from1, from3, second, wh))
        second = send(second, SWAP)
        a3 = send(one(third_kernel, own, a3, first, a4), along_z(1))
        g1t, g3b = call(
            side_doc_kernel, [(chip, f32)] * 2, [place, wh, wl, qh, ql, from1, from3]
        )
        y1t, y3b = send(g1t, along_second(1)), send(g3b, along_second(-1))
        a2, b2, a1, b1, near = call(
            second_kernel, [(own, f32)] * 5, [place, a2, b2, a1, b1, near, second]
        )
        b2 = send(one(sum_kernel, own, b2, b3), along_z(1))
        g0 = one(near_doc_kernel, block, wh, wl, qh, ql)
        a3, g0 = together((a3, g0))
        a2 = send(one(sum_kernel, own, a2, a3), along_z(1))
        b1 = send(one(sum_kernel, own, b1, b2), along_z(1))
        d0, d1, d2, d3 = call(fold_kernel, [(own, f32)] * 4, [place, g0, y1t, y1b, y3t, y3b])
        d1, d2, d3 = (
            send(d1, along_first(1)),
            send(d2, along_first(2)),
            send(d3, along_first(-1)),
        )
        a1 = send(one(sum_kernel, own, a1, a2), along_z(1))
        grad_doc = d0 + d1 + d2 + d3
        grad_query = near + a1 + send(b1, SWAP)
    row_loss = lax.dynamic_slice(losses[0], (z * CHIP + c * OWN,), (OWN,))
    col_loss = lax.dynamic_slice(losses[1], ((y * 4 + x) * OWN,), (OWN,))
    return row_loss, col_loss, grad_query, grad_doc


def solution(mesh):
    rows, flat_rows = P(AXES, None), P(AXES)
    return jax.shard_map(
        body,
        mesh=mesh,
        in_specs=(rows, rows, flat_rows),
        out_specs=(flat_rows, flat_rows, rows, rows),
        check_vma=False,
    )
```

```python
import functools

import jax
import jax.numpy as jnp
from jax import lax
from jax.experimental import pallas as pl
from jax.experimental.pallas import tpu as pltpu
from jax.sharding import PartitionSpec as P

inv_temp = 20.0
f32, bf16 = jnp.float32, jnp.bfloat16
AXES = ("loop", "grp")
OWN = 64
CHIP = 2 * OWN
PIECE = OWN + 8
WIDE = 1024
BLOCK = 256
EARLY_Q, EARLY_D = 640, 768
VMEM_LIMIT = 12 * 1024 * 1024
GROUPS = ((0, 0), (0, 2), (1, 0), (3, 2), (1, 2), (3, 0), (2, 0), (2, 2))


def flat(x, y, z, c):
    return (((y & 1) * 8 + z) * 2 + c) * 8 + (y >> 1) * 4 + x


def permutation(move):
    return [
        (flat(x, y, z, c), flat(*move(x, y, z, c)))
        for x in range(4)
        for y in range(4)
        for z in range(8)
        for c in range(2)
    ]


def along_first(delta):
    return permutation(
        lambda x, y, z, c: ((x + delta) % 4, y, z, c) if c == 0 else (x, (y + delta) % 4, z, c)
    )


def along_second(delta):
    return permutation(
        lambda x, y, z, c: (x, (y + delta) % 4, z, c) if c == 0 else ((x + delta) % 4, y, z, c)
    )


def along_z(delta):
    return permutation(
        lambda x, y, z, c: (x, y, (z + delta) % 8, c) if c == 0 else (x, y, (z - delta) % 8, c)
    )


SWAP = permutation(lambda x, y, z, c: (x, y, z, 1 - c))


def send(value, perm):
    return lax.ppermute(value, AXES, perm)


together = lax.optimization_barrier


def split(value):
    high = value.astype(bf16)
    return high, (value - high.astype(f32)).astype(bf16)


def dot3(ah, al, bh, bl, dims):
    dot = functools.partial(
        lax.dot_general, dimension_numbers=(dims, ((), ())), preferred_element_type=f32
    )
    return dot(ah, bh) + dot(ah, bl) + dot(al, bh)


def call(kernel, shapes, inputs, scratch=(), aliases=()):
    held = [pltpu.with_memory_space_constraint(a, pltpu.VMEM) for a in inputs[1:]]
    return pl.pallas_call(
        kernel,
        out_shape=[pltpu.VMEM(s, t) for s, t in shapes],
        in_specs=[pl.BlockSpec(memory_space=pltpu.SMEM)]
        + [pl.BlockSpec(memory_space=pltpu.VMEM)] * len(held),
        out_specs=[pl.BlockSpec(memory_space=pltpu.VMEM)] * len(shapes),
        scratch_shapes=list(scratch),
        input_output_aliases=dict(aliases),
        compiler_params=pltpu.CompilerParams(vmem_limit_bytes=VMEM_LIMIT),
    )(inputs[0], *held)


def block_z(z, c, block):
    sign = 1 - 2 * c
    steps = (0, 1, -1, 2, -2, 3, -3, 4)[block]
    return (z + sign * steps) & 7


def doc_chip(x, y, c, first, second):
    dx = jnp.where(c == 0, first, second)
    dy = jnp.where(c == 0, second, first)
    return ((y + dy) & 3) * 4 + ((x + dx) & 3)


def doc_piece(x, y, c, piece):
    second, first = GROUPS[piece // 2]
    return doc_chip(x, y, c, first + piece % 2, second)


def doc_ids(block, x, y, z, c):
    row = lax.broadcasted_iota(jnp.int32, (OWN, 1), 0)
    ids = []
    for piece in range(block * 4, block * 4 + 4):
        chip = doc_piece(x, y, c, piece)
        ids.append(row + flat(chip & 3, chip >> 2, z, c) * OWN)
    return jnp.concatenate(ids, axis=0).astype(f32)


def put(high, low, ref, start, count, row):
    h, l = split(ref[start : start + count, :])
    high[row : row + count, :] = h
    low[row : row + count, :] = l


def pack_kernel(place, query, pairs, out):
    out[0:OWN, :] = query[...]
    out[OWN:, :] = jnp.zeros((8, WIDE), f32)
    out[OWN : OWN + 1, :OWN] = pairs[...]


def stack_kernel(place, *refs):
    for k, ref in enumerate(refs[:-1]):
        refs[-1][k * PIECE : (k + 1) * PIECE, :] = ref[...]


def put_queries(qh, ql, pair, block, mine, mine_at, other, other_at):
    put(qh, ql, mine, mine_at, OWN, block * CHIP)
    put(qh, ql, other, other_at, OWN, block * CHIP + OWN)
    first = mine[mine_at + OWN : mine_at + PIECE, :CHIP]
    last = other[other_at + OWN : other_at + PIECE, :CHIP]
    pair[:, block * CHIP : (block + 1) * CHIP] = first + pltpu.roll(last, OWN, 1)


def early_kernel(place, u, uo, a1, b1, a2, b2, s12, p1t, p1b, r1t, r1b, r3t, r3b, *outs):
    st, qh, ql, dh, dl, pair = outs
    put_queries(qh, ql, pair, 0, u, 0, uo, 0)
    put_queries(qh, ql, pair, 1, a1, 0, b1, 0)
    put_queries(qh, ql, pair, 2, s12, PIECE, s12, 0)
    put_queries(qh, ql, pair, 3, a2, 0, b2, 0)
    put_queries(qh, ql, pair, 4, s12, 3 * PIECE, s12, 2 * PIECE)
    for k, ref in enumerate((p1t, p1b, r1t, r3b, r1b, r3t)):
        put(dh, dl, ref, 0, CHIP, k * CHIP)
    q = slice(0, EARLY_Q)
    for b in range(3):
        at = slice(b * BLOCK, (b + 1) * BLOCK)
        s = dot3(dh[at, :], dl[at, :], qh[q, :], ql[q, :], ((1,), (1,)))
        st[at, q] = s * inv_temp


def score_kernel(place, a3, b3, a4, s34, r2t, r2b, *refs):
    st, qh, ql, dh, dl, pair, keep, give, mixed = refs[6:]
    x, y, z, c = place[0], place[1], place[2], place[3]
    put_queries(qh, ql, pair, 5, a3, 0, b3, 0)
    put_queries(qh, ql, pair, 6, s34, PIECE, s34, 0)
    put_queries(qh, ql, pair, 7, a4, 0, s34, 2 * PIECE)
    put(dh, dl, r2t, 0, CHIP, EARLY_D)
    put(dh, dl, r2b, 0, CHIP, EARLY_D + CHIP)
    pairs = pair[0:1, :]
    lane = lax.broadcasted_iota(jnp.int32, (BLOCK, 128), 1)
    for b in range(4):
        at = slice(b * BLOCK, (b + 1) * BLOCK)
        q = slice(EARLY_Q if b < 3 else 0, WIDE)
        s = dot3(dh[at, :], dl[at, :], qh[q, :], ql[q, :], ((1,), (1,)))
        st[at, q] = s * inv_temp
        s = st[at, :]
        picked = jnp.where(pairs == doc_ids(b, x, y, z, c), s, 0.0)
        cm = jnp.max(s, axis=1, keepdims=True)
        ce = jnp.sum(jnp.exp(s - cm), axis=1, keepdims=True)
        cp = jnp.sum(picked, axis=1, keepdims=True)
        stats = jnp.where(lane == 0, cm, jnp.where(lane == 1, ce, cp))
        for a in range(4):
            row = pl.multiple_of(doc_piece(x, y, c, b * 4 + a) * OWN, OWN)
            mixed[pl.ds(row, OWN), :] = stats[a * OWN : (a + 1) * OWN, :]
        bm = jnp.max(s, axis=0, keepdims=True)
        bp = jnp.sum(picked, axis=0, keepdims=True)
        if b == 0:
            rm, rp = bm, bp
            re = jnp.sum(jnp.exp(s - rm), axis=0, keepdims=True)
        else:
            top = jnp.maximum(rm, bm)
            re = re * jnp.exp(rm - top) + jnp.sum(jnp.exp(s - top), axis=0, keepdims=True)
            rm, rp = top, rp + bp
    rows = jnp.concatenate([rm, re, rp, jnp.zeros((5, WIDE), f32)], axis=0)

    def put_stats(row_out, col_out):
        for block in range(8):
            part = rows[:, block * CHIP : (block + 1) * CHIP]
            part = jnp.where(c == 0, part, pltpu.roll(part, OWN, 1))
            at = pl.multiple_of(block_z(z, c, block) * CHIP, CHIP)
            row_out[:, pl.ds(at, CHIP)] = part
        for b in range(4):
            at = slice(b * BLOCK, (b + 1) * BLOCK)
            col_out[:, at] = mixed[at, :].T[0:8, :]

    @pl.when(c == 0)
    def _():
        put_stats(keep, give)

    @pl.when(c == 1)
    def _():
        put_stats(give, keep)


def combine(a, b):
    top = jnp.maximum(a[0:1, :], b[0:1, :])
    total = a[1:2, :] * jnp.exp(a[0:1, :] - top) + b[1:2, :] * jnp.exp(b[0:1, :] - top)
    return jnp.concatenate(
        [top, total, a[2:3, :] + b[2:3, :], jnp.zeros((5, WIDE), f32)], axis=0
    )


def merge_kernel(place, keep, got, state):
    mine, theirs = keep[...], got[...]
    both = combine(mine, theirs)
    state[0:8, :] = jnp.where(place[3] == 0, both, mine)
    state[8:16, :] = jnp.where(place[3] == 0, both, theirs)


def round_kernel(place, state, got, out):
    out[0:8, :] = combine(state[0:8, :], got[0:8, :])
    out[8:16, :] = combine(state[8:16, :], got[8:16, :])


def last_round_kernel(place, state, got, mine, give):
    for out, at in ((mine, slice(0, 8)), (give, slice(8, 16))):
        so_far = state[at, :]
        out[...] = jnp.where(place[3] == 0, so_far, combine(so_far, got[at, :]))


def sum_kernel(place, *refs):
    *parts, out = refs
    out[...] = sum((part[...] for part in parts[1:]), parts[0][...])


def query_products(wh, wl, dh, dl, lo, hi):
    return dot3(wh[:, lo:hi], wl[:, lo:hi], dh[...], dl[...], ((0,), (0,)))


def weight_kernel(place, st, pair, mine, got, dh, dl, *refs):
    wh, wl, a4, a3, b3, first, losses, lse, columns = refs
    x, y, z, c = place[0], place[1], place[2], place[3]
    row_stats = jnp.where(c == 0, mine[...], got[...])
    col_stats = jnp.where(c == 0, got[...], mine[...])
    row_lse = row_stats[0:1, :] + jnp.log(row_stats[1:2, :])
    col_lse = col_stats[0:1, :] + jnp.log(col_stats[1:2, :])
    losses[...] = jnp.concatenate(
        [row_lse - row_stats[2:3, :], col_lse - col_stats[2:3, :], jnp.zeros((6, WIDE), f32)],
        axis=0,
    )
    lse[...] = jnp.broadcast_to(row_lse, (8, WIDE))
    parts = []
    for block in range(8):
        at = pl.multiple_of(block_z(z, c, block) * CHIP, CHIP)
        part = lse[:, pl.ds(at, CHIP)]
        parts.append(jnp.where(c == 0, part, pltpu.roll(part, OWN, 1)))
    row_lse = jnp.concatenate(parts, axis=1)[0:1, :]
    for b in range(4):
        at = slice(b * BLOCK, (b + 1) * BLOCK)
        columns[at, :] = jnp.broadcast_to(col_lse[:, at], (128, BLOCK)).T
    pairs = pair[0:1, :]
    for b in range(4):
        at = slice(b * BLOCK, (b + 1) * BLOCK)
        s = st[at, :]
        parts = []
        for a in range(4):
            row = pl.multiple_of(doc_piece(x, y, c, b * 4 + a) * OWN, OWN)
            parts.append(columns[pl.ds(row, OWN), :])
        cl = jnp.concatenate(parts, axis=0)[:, 0:1]
        w = (jnp.exp(s - row_lse) + jnp.exp(s - cl)) * (0.5 * inv_temp)
        w = w - jnp.where(pairs == doc_ids(b, x, y, z, c), inv_temp, 0.0)
        h, l = split(w)
        wh[at, :] = h
        wl[at, :] = l
    g = query_products(wh, wl, dh, dl, EARLY_Q, WIDE)
    a3[...] = g[:OWN]
    b3[...] = g[OWN:CHIP]
    a4[...] = g[2 * CHIP : 2 * CHIP + OWN]
    first[0:OWN, :] = g[2 * CHIP + OWN :]
    first[OWN : 2 * OWN, :] = g[CHIP + OWN : 2 * CHIP]
    first[2 * OWN :, :] = g[CHIP : CHIP + OWN]


def first_kernel(place, a4, b3, first, a4_out, b3_out):
    a4_out[...] = a4[...] + first[0:OWN, :]
    b3_out[...] = b3[...] + first[2 * OWN :, :]


def third_kernel(place, a3, first, from4, out):
    out[...] = a3[...] + first[OWN : 2 * OWN, :] + from4[...]


def query_kernel(place, wh, wl, dh, dl, a2, b2, a1, b1, near, second):
    g = query_products(wh, wl, dh, dl, 0, EARLY_Q)
    near[...] = g[:OWN]
    a1[...] = g[CHIP : CHIP + OWN]
    b1[...] = g[CHIP + OWN : 2 * CHIP]
    a2[...] = g[3 * CHIP : 3 * CHIP + OWN]
    b2[...] = g[3 * CHIP + OWN : 4 * CHIP]
    second[0:OWN, :] = g[4 * CHIP + OWN :]
    second[OWN : 2 * OWN, :] = g[4 * CHIP : 4 * CHIP + OWN]
    second[2 * OWN : 3 * OWN, :] = g[2 * CHIP + OWN : 3 * CHIP]
    second[3 * OWN : 4 * OWN, :] = g[2 * CHIP : 2 * CHIP + OWN]
    second[4 * OWN :, :] = g[OWN:CHIP]


def second_kernel(place, a2, b2, a1, b1, near, second, a2_out, b2_out, a1_out, b1_out, near_out):
    pairs = ((a2, a2_out), (b2, b2_out), (a1, a1_out), (b1, b1_out), (near, near_out))
    for k, (part, out) in enumerate(pairs):
        out[...] = part[...] + second[k * OWN : (k + 1) * OWN, :]


def doc_products(wh, wl, qh, ql, lo, hi):
    return dot3(wh[lo:hi, :], wl[lo:hi, :], qh[...], ql[...], ((1,), (0,)))


def far_doc_kernel(place, wh, wl, qh, ql, g1b, g3t, g2t, g2b):
    g = doc_products(wh, wl, qh, ql, 2 * BLOCK, WIDE)
    for k, out in enumerate((g1b, g3t, g2t, g2b)):
        out[...] = g[k * CHIP : (k + 1) * CHIP]


def side_doc_kernel(place, wh, wl, qh, ql, from1, from3, g1t, g3b):
    g = doc_products(wh, wl, qh, ql, BLOCK, 2 * BLOCK)
    g1t[...] = g[:CHIP] + from1[...]
    g3b[...] = g[CHIP:] + from3[...]


def near_doc_kernel(place, wh, wl, qh, ql, g0):
    g0[...] = doc_products(wh, wl, qh, ql, 0, BLOCK)


def fold_kernel(place, g0, y1t, y1b, y3t, y3b, d0, d1, d2, d3):
    for k, out in enumerate((d0, d1, d2, d3)):
        half = slice(k % 2 * OWN, (k % 2 + 1) * OWN)
        one, three = (y1t, y3t) if k < 2 else (y1b, y3b)
        out[...] = g0[k * OWN : (k + 1) * OWN, :] + one[half, :] + three[half, :]


def next_over(k, size):
    return (k + 1) % size if k % 2 else (k - 1) % size


def body(query, document, pair_index):
    loop, grp = lax.axis_index("loop"), lax.axis_index("grp")
    c, z = loop & 1, (loop >> 1) & 7
    x, y = grp & 3, (grp >> 2) * 2 + (loop >> 4)
    place = jnp.stack([x, y, z, c]).astype(jnp.int32)
    square = (WIDE, WIDE)
    piece, chip, block = (PIECE, WIDE), (CHIP, WIDE), (BLOCK, WIDE)
    own, totals = (OWN, WIDE), (8, WIDE)

    def one(kernel, shape, *inputs):
        return call(kernel, [(shape, f32)], [place, *inputs])[0]

    with jax.named_scope("gather"):
        d1, d3 = send(document, along_first(-1)), send(document, along_first(1))
        d2 = send(document, along_first(-2))
        u = one(pack_kernel, piece, query, pair_index.astype(f32)[None, :])
        uo = send(u, SWAP)
        a1 = send(u, along_z(-1))
        p1t = jnp.concatenate([document, d1])
        uo, p1t = together((uo, p1t))
        b1 = send(uo, along_z(-1))
        r1t, r3t = send(p1t, along_second(-1)), send(p1t, along_second(1))
        p1b = jnp.concatenate([d2, d3])
        a1, p1b = together((a1, p1b))
        a2 = send(a1, along_z(-1))
        r1b, r3b = send(p1b, along_second(-1)), send(p1b, along_second(1))
        b1, r1t, r3t = together((b1, r1t, r3t))
        b2 = send(b1, along_z(-1))
        r2t = send(r1t, along_second(-1))
        a2, r1b, r3b = together((a2, r1b, r3b))
        a3 = send(a2, along_z(-1))
        r2b = send(r3b, along_second(1))
        b3 = send(b2, along_z(-1))
        s12 = send(one(stack_kernel, (4 * PIECE, WIDE), a1, b1, a2, b2), SWAP)
        a3, r2t = together((a3, r2t))
        a4 = send(a3, along_z(-1))
        b3, r2b = together((b3, r2b))
        s34 = send(one(stack_kernel, (3 * PIECE, WIDE), a3, b3, a4), SWAP)
    tile = [(square, f32)] + [(square, bf16)] * 4 + [(totals, f32)]
    held = call(
        early_kernel,
        tile,
        [place, u, uo, a1, b1, a2, b2, s12, p1t, p1b, r1t, r1b, r3t, r3b],
    )
    st, qh, ql, dh, dl, pair, keep, give = call(
        score_kernel,
        tile + [(totals, f32)] * 2,
        [place, a3, b3, a4, s34, r2t, r2b, *held],
        [pltpu.VMEM((WIDE, 128), f32)],
        aliases=[(7 + k, k) for k in range(6)],
    )
    with jax.named_scope("totals"):
        state = one(merge_kernel, (16, WIDE), keep, send(give, SWAP))
        third_z = (3, 6, 5, 0, 7, 2, 1, 4)
        for move in (
            lambda x, y, z, c: (x, y, z ^ 1, c) if c == 0 else (x ^ 1, y, z, c),
            lambda x, y, z, c: (x, y, next_over(z, 8), c) if c == 0 else (next_over(x, 4), y, z, c),
            lambda x, y, z, c: (x, y, third_z[z], c) if c == 0 else (x, y ^ 1, z, c),
        ):
            state = one(round_kernel, (16, WIDE), state, send(state, permutation(move)))
        last = [
            (source, target)
            for source, target in permutation(lambda x, y, z, c: (x, next_over(y, 4), z, c))
            if source // 8 % 2 == 1
        ]
        mine, give = call(
            last_round_kernel, [(totals, f32)] * 2, [place, state, send(state, last)]
        )
        got = send(give, SWAP)
    wh, wl, a4, a3, b3, first, losses = call(
        weight_kernel,
        [(square, bf16)] * 2 + [(own, f32)] * 3 + [((3 * OWN, WIDE), f32), (totals, f32)],
        [place, st, pair, mine, got, dh, dl],
        [pltpu.VMEM((8, WIDE), f32), pltpu.VMEM((WIDE, 128), f32)],
    )
    with jax.named_scope("scatter"):
        first = send(first, SWAP)
        g1b, g3t, g2t, g2b = call(far_doc_kernel, [(chip, f32)] * 4, [place, wh, wl, qh, ql])
        first, g1b, g3t, g2t, g2b, wh = together((first, g1b, g3t, g2t, g2b, wh))
        a4, b3 = call(first_kernel, [(own, f32)] * 2, [place, a4, b3, first])
        a4, b3, wh = together((a4, b3, wh))
        from1, from3 = send(g2t, along_second(1)), send(g2b, along_second(-1))
        a4, b3 = send(a4, along_z(1)), send(b3, along_z(1))
        y1b, y3t = send(g1b, along_second(1)), send(g3t, along_second(-1))
        a2, b2, a1, b1, near, second = call(
            query_kernel,
            [(own, f32)] * 5 + [((5 * OWN, WIDE), f32)],
            [place, wh, wl, dh, dl],
        )
        a4, b3, from1, from3, second, wh = together((a4, b3, from1, from3, second, wh))
        second = send(second, SWAP)
        a3 = send(one(third_kernel, own, a3, first, a4), along_z(1))
        g1t, g3b = call(
            side_doc_kernel, [(chip, f32)] * 2, [place, wh, wl, qh, ql, from1, from3]
        )
        y1t, y3b = send(g1t, along_second(1)), send(g3b, along_second(-1))
        a2, b2, a1, b1, near = call(
            second_kernel, [(own, f32)] * 5, [place, a2, b2, a1, b1, near, second]
        )
        b2 = send(one(sum_kernel, own, b2, b3), along_z(1))
        g0 = one(near_doc_kernel, block, wh, wl, qh, ql)
        a3, g0 = together((a3, g0))
        a2 = send(one(sum_kernel, own, a2, a3), along_z(1))
        b1 = send(one(sum_kernel, own, b1, b2), along_z(1))
        d0, d1, d2, d3 = call(fold_kernel, [(own, f32)] * 4, [place, g0, y1t, y1b, y3t, y3b])
        d1, d2, d3 = (
            send(d1, along_first(1)),
            send(d2, along_first(2)),
            send(d3, along_first(-1)),
        )
        a1 = send(one(sum_kernel, own, a1, a2), along_z(1))
        grad_doc = d0 + d1 + d2 + d3
        grad_query = near + a1 + send(b1, SWAP)
    row_loss = lax.dynamic_slice(losses[0], (z * CHIP + c * OWN,), (OWN,))
    col_loss = lax.dynamic_slice(losses[1], ((y * 4 + x) * OWN,), (OWN,))
    return row_loss, col_loss, grad_query, grad_doc


def solution(mesh):
    rows, flat_rows = P(AXES, None), P(AXES)
    return jax.shard_map(
        body,
        mesh=mesh,
        in_specs=(rows, rows, flat_rows),
        out_specs=(flat_rows, flat_rows, rows, rows),
        check_vma=False,
    )
```

```python
import functools

import jax
import jax.numpy as jnp
from jax import lax
from jax.experimental import pallas as pl
from jax.experimental.pallas import tpu as pltpu
from jax.sharding import PartitionSpec as P

inv_temp = 20.0
f32, bf16 = jnp.float32, jnp.bfloat16
AXES = ("loop", "grp")
OWN = 64
CHIP = 2 * OWN
PIECE = OWN + 8
WIDE = 1024
BLOCK = 256
EARLY_Q, EARLY_D = 640, 768
VMEM_LIMIT = 12 * 1024 * 1024
GROUPS = ((0, 0), (0, 2), (1, 0), (3, 2), (1, 2), (3, 0), (2, 0), (2, 2))


def flat(x, y, z, c):
    return (((y & 1) * 8 + z) * 2 + c) * 8 + (y >> 1) * 4 + x


def permutation(move):
    return [
        (flat(x, y, z, c), flat(*move(x, y, z, c)))
        for x in range(4)
        for y in range(4)
        for z in range(8)
        for c in range(2)
    ]


def along_first(delta):
    return permutation(
        lambda x, y, z, c: ((x + delta) % 4, y, z, c) if c == 0 else (x, (y + delta) % 4, z, c)
    )


def along_second(delta):
    return permutation(
        lambda x, y, z, c: (x, (y + delta) % 4, z, c) if c == 0 else ((x + delta) % 4, y, z, c)
    )


def along_z(delta):
    return permutation(
        lambda x, y, z, c: (x, y, (z + delta) % 8, c) if c == 0 else (x, y, (z - delta) % 8, c)
    )


SWAP = permutation(lambda x, y, z, c: (x, y, z, 1 - c))


def send(value, perm):
    return lax.ppermute(value, AXES, perm)


together = lax.optimization_barrier


def split(value):
    high = value.astype(bf16)
    return high, (value - high.astype(f32)).astype(bf16)


def dot3(ah, al, bh, bl, dims):
    dot = functools.partial(
        lax.dot_general, dimension_numbers=(dims, ((), ())), preferred_element_type=f32
    )
    return dot(ah, bh) + dot(ah, bl) + dot(al, bh)


def call(kernel, shapes, inputs, scratch=(), aliases=()):
    held = [pltpu.with_memory_space_constraint(a, pltpu.VMEM) for a in inputs[1:]]
    return pl.pallas_call(
        kernel,
        out_shape=[pltpu.VMEM(s, t) for s, t in shapes],
        in_specs=[pl.BlockSpec(memory_space=pltpu.SMEM)]
        + [pl.BlockSpec(memory_space=pltpu.VMEM)] * len(held),
        out_specs=[pl.BlockSpec(memory_space=pltpu.VMEM)] * len(shapes),
        scratch_shapes=list(scratch),
        input_output_aliases=dict(aliases),
        compiler_params=pltpu.CompilerParams(vmem_limit_bytes=VMEM_LIMIT),
    )(inputs[0], *held)


def block_z(z, c, block):
    sign = 1 - 2 * c
    steps = (0, 1, -1, 2, -2, 3, -3, 4)[block]
    return (z + sign * steps) & 7


def doc_chip(x, y, c, first, second):
    dx = jnp.where(c == 0, first, second)
    dy = jnp.where(c == 0, second, first)
    return ((y + dy) & 3) * 4 + ((x + dx) & 3)


def doc_piece(x, y, c, piece):
    second, first = GROUPS[piece // 2]
    return doc_chip(x, y, c, first + piece % 2, second)


def doc_ids(block, x, y, z, c):
    row = lax.broadcasted_iota(jnp.int32, (OWN, 1), 0)
    ids = []
    for piece in range(block * 4, block * 4 + 4):
        chip = doc_piece(x, y, c, piece)
        ids.append(row + flat(chip & 3, chip >> 2, z, c) * OWN)
    return jnp.concatenate(ids, axis=0).astype(f32)


def put(high, low, ref, start, count, row):
    h, l = split(ref[start : start + count, :])
    high[row : row + count, :] = h
    low[row : row + count, :] = l


def pack_kernel(place, query, pairs, out):
    out[0:OWN, :] = query[...]
    out[OWN:, :] = jnp.zeros((8, WIDE), f32)
    out[OWN : OWN + 1, :OWN] = pairs[...]


def stack_kernel(place, *refs):
    for k, ref in enumerate(refs[:-1]):
        refs[-1][k * PIECE : (k + 1) * PIECE, :] = ref[...]


def put_queries(qh, ql, pair, block, mine, mine_at, other, other_at):
    put(qh, ql, mine, mine_at, OWN, block * CHIP)
    put(qh, ql, other, other_at, OWN, block * CHIP + OWN)
    first = mine[mine_at + OWN : mine_at + PIECE, :CHIP]
    last = other[other_at + OWN : other_at + PIECE, :CHIP]
    pair[:, block * CHIP : (block + 1) * CHIP] = first + pltpu.roll(last, OWN, 1)


def early_kernel(place, u, uo, a1, b1, a2, b2, s12, p1t, p1b, r1t, r1b, r3t, r3b, *outs):
    st, qh, ql, dh, dl, pair = outs
    put_queries(qh, ql, pair, 0, u, 0, uo, 0)
    put_queries(qh, ql, pair, 1, a1, 0, b1, 0)
    put_queries(qh, ql, pair, 2, s12, PIECE, s12, 0)
    put_queries(qh, ql, pair, 3, a2, 0, b2, 0)
    put_queries(qh, ql, pair, 4, s12, 3 * PIECE, s12, 2 * PIECE)
    for k, ref in enumerate((p1t, p1b, r1t, r3b, r1b, r3t)):
        put(dh, dl, ref, 0, CHIP, k * CHIP)
    q = slice(0, EARLY_Q)
    for b in range(3):
        at = slice(b * BLOCK, (b + 1) * BLOCK)
        s = dot3(dh[at, :], dl[at, :], qh[q, :], ql[q, :], ((1,), (1,)))
        st[at, q] = s * inv_temp


def score_kernel(place, a3, b3, a4, s34, r2t, r2b, *refs):
    st, qh, ql, dh, dl, pair, keep, give, mixed = refs[6:]
    x, y, z, c = place[0], place[1], place[2], place[3]
    put_queries(qh, ql, pair, 5, a3, 0, b3, 0)
    put_queries(qh, ql, pair, 6, s34, PIECE, s34, 0)
    put_queries(qh, ql, pair, 7, a4, 0, s34, 2 * PIECE)
    put(dh, dl, r2t, 0, CHIP, EARLY_D)
    put(dh, dl, r2b, 0, CHIP, EARLY_D + CHIP)
    pairs = pair[0:1, :]
    lane = lax.broadcasted_iota(jnp.int32, (BLOCK, 128), 1)
    for b in range(4):
        at = slice(b * BLOCK, (b + 1) * BLOCK)
        q = slice(EARLY_Q if b < 3 else 0, WIDE)
        s = dot3(dh[at, :], dl[at, :], qh[q, :], ql[q, :], ((1,), (1,)))
        st[at, q] = s * inv_temp
        s = st[at, :]
        picked = jnp.where(pairs == doc_ids(b, x, y, z, c), s, 0.0)
        cm = jnp.max(s, axis=1, keepdims=True)
        ce = jnp.sum(jnp.exp(s - cm), axis=1, keepdims=True)
        cp = jnp.sum(picked, axis=1, keepdims=True)
        stats = jnp.where(lane == 0, cm, jnp.where(lane == 1, ce, cp))
        for a in range(4):
            row = pl.multiple_of(doc_piece(x, y, c, b * 4 + a) * OWN, OWN)
            mixed[pl.ds(row, OWN), :] = stats[a * OWN : (a + 1) * OWN, :]
        bm = jnp.max(s, axis=0, keepdims=True)
        bp = jnp.sum(picked, axis=0, keepdims=True)
        if b == 0:
            rm, rp = bm, bp
            re = jnp.sum(jnp.exp(s - rm), axis=0, keepdims=True)
        else:
            top = jnp.maximum(rm, bm)
            re = re * jnp.exp(rm - top) + jnp.sum(jnp.exp(s - top), axis=0, keepdims=True)
            rm, rp = top, rp + bp
    rows = jnp.concatenate([rm, re, rp, jnp.zeros((5, WIDE), f32)], axis=0)

    def put_stats(row_out, col_out):
        for block in range(8):
            part = rows[:, block * CHIP : (block + 1) * CHIP]
            part = jnp.where(c == 0, part, pltpu.roll(part, OWN, 1))
            at = pl.multiple_of(block_z(z, c, block) * CHIP, CHIP)
            row_out[:, pl.ds(at, CHIP)] = part
        for b in range(4):
            at = slice(b * BLOCK, (b + 1) * BLOCK)
            col_out[:, at] = mixed[at, :].T[0:8, :]

    @pl.when(c == 0)
    def _():
        put_stats(keep, give)

    @pl.when(c == 1)
    def _():
        put_stats(give, keep)


def combine(a, b):
    top = jnp.maximum(a[0:1, :], b[0:1, :])
    total = a[1:2, :] * jnp.exp(a[0:1, :] - top) + b[1:2, :] * jnp.exp(b[0:1, :] - top)
    return jnp.concatenate(
        [top, total, a[2:3, :] + b[2:3, :], jnp.zeros((5, WIDE), f32)], axis=0
    )


def merge_kernel(place, keep, got, state):
    mine, theirs = keep[...], got[...]
    both = combine(mine, theirs)
    state[0:8, :] = jnp.where(place[3] == 0, both, mine)
    state[8:16, :] = jnp.where(place[3] == 0, both, theirs)


def round_kernel(place, state, got, out):
    out[0:8, :] = combine(state[0:8, :], got[0:8, :])
    out[8:16, :] = combine(state[8:16, :], got[8:16, :])


def last_round_kernel(place, state, got, mine, give):
    for out, at in ((mine, slice(0, 8)), (give, slice(8, 16))):
        so_far = state[at, :]
        out[...] = jnp.where(place[3] == 0, so_far, combine(so_far, got[at, :]))


def sum_kernel(place, *refs):
    *parts, out = refs
    out[...] = sum((part[...] for part in parts[1:]), parts[0][...])


def query_products(wh, wl, dh, dl, lo, hi):
    return dot3(wh[:, lo:hi], wl[:, lo:hi], dh[...], dl[...], ((0,), (0,)))


def weight_kernel(place, st, pair, mine, got, dh, dl, *refs):
    wh, wl, a4, a3, b3, first, losses, lse, columns = refs
    x, y, z, c = place[0], place[1], place[2], place[3]
    row_stats = jnp.where(c == 0, mine[...], got[...])
    col_stats = jnp.where(c == 0, got[...], mine[...])
    row_lse = row_stats[0:1, :] + jnp.log(row_stats[1:2, :])
    col_lse = col_stats[0:1, :] + jnp.log(col_stats[1:2, :])
    losses[...] = jnp.concatenate(
        [row_lse - row_stats[2:3, :], col_lse - col_stats[2:3, :], jnp.zeros((6, WIDE), f32)],
        axis=0,
    )
    lse[...] = jnp.broadcast_to(row_lse, (8, WIDE))
    parts = []
    for block in range(8):
        at = pl.multiple_of(block_z(z, c, block) * CHIP, CHIP)
        part = lse[:, pl.ds(at, CHIP)]
        parts.append(jnp.where(c == 0, part, pltpu.roll(part, OWN, 1)))
    row_lse = jnp.concatenate(parts, axis=1)[0:1, :]
    for b in range(4):
        at = slice(b * BLOCK, (b + 1) * BLOCK)
        columns[at, :] = jnp.broadcast_to(col_lse[:, at], (128, BLOCK)).T
    pairs = pair[0:1, :]
    for b in range(4):
        at = slice(b * BLOCK, (b + 1) * BLOCK)
        s = st[at, :]
        parts = []
        for a in range(4):
            row = pl.multiple_of(doc_piece(x, y, c, b * 4 + a) * OWN, OWN)
            parts.append(columns[pl.ds(row, OWN), :])
        cl = jnp.concatenate(parts, axis=0)[:, 0:1]
        w = (jnp.exp(s - row_lse) + jnp.exp(s - cl)) * (0.5 * inv_temp)
        w = w - jnp.where(pairs == doc_ids(b, x, y, z, c), inv_temp, 0.0)
        h, l = split(w)
        wh[at, :] = h
        wl[at, :] = l
    g = query_products(wh, wl, dh, dl, EARLY_Q, WIDE)
    a3[...] = g[:OWN]
    b3[...] = g[OWN:CHIP]
    a4[...] = g[2 * CHIP : 2 * CHIP + OWN]
    first[0:OWN, :] = g[2 * CHIP + OWN :]
    first[OWN : 2 * OWN, :] = g[CHIP + OWN : 2 * CHIP]
    first[2 * OWN :, :] = g[CHIP : CHIP + OWN]


def first_kernel(place, a4, b3, first, a4_out, b3_out):
    a4_out[...] = a4[...] + first[0:OWN, :]
    b3_out[...] = b3[...] + first[2 * OWN :, :]


def third_kernel(place, a3, first, from4, out):
    out[...] = a3[...] + first[OWN : 2 * OWN, :] + from4[...]


def query_kernel(place, wh, wl, dh, dl, a2, b2, a1, b1, near, second):
    g = query_products(wh, wl, dh, dl, 0, EARLY_Q)
    near[...] = g[:OWN]
    a1[...] = g[CHIP : CHIP + OWN]
    b1[...] = g[CHIP + OWN : 2 * CHIP]
    a2[...] = g[3 * CHIP : 3 * CHIP + OWN]
    b2[...] = g[3 * CHIP + OWN : 4 * CHIP]
    second[0:OWN, :] = g[4 * CHIP + OWN :]
    second[OWN : 2 * OWN, :] = g[4 * CHIP : 4 * CHIP + OWN]
    second[2 * OWN : 3 * OWN, :] = g[2 * CHIP + OWN : 3 * CHIP]
    second[3 * OWN : 4 * OWN, :] = g[2 * CHIP : 2 * CHIP + OWN]
    second[4 * OWN :, :] = g[OWN:CHIP]


def second_kernel(place, a2, b2, a1, b1, near, second, a2_out, b2_out, a1_out, b1_out, near_out):
    pairs = ((a2, a2_out), (b2, b2_out), (a1, a1_out), (b1, b1_out), (near, near_out))
    for k, (part, out) in enumerate(pairs):
        out[...] = part[...] + second[k * OWN : (k + 1) * OWN, :]


def doc_products(wh, wl, qh, ql, lo, hi):
    return dot3(wh[lo:hi, :], wl[lo:hi, :], qh[...], ql[...], ((1,), (0,)))


def far_doc_kernel(place, wh, wl, qh, ql, g1b, g3t, g2t, g2b):
    g = doc_products(wh, wl, qh, ql, 2 * BLOCK, WIDE)
    for k, out in enumerate((g1b, g3t, g2t, g2b)):
        out[...] = g[k * CHIP : (k + 1) * CHIP]


def side_doc_kernel(place, wh, wl, qh, ql, from1, from3, g1t, g3b):
    g = doc_products(wh, wl, qh, ql, BLOCK, 2 * BLOCK)
    g1t[...] = g[:CHIP] + from1[...]
    g3b[...] = g[CHIP:] + from3[...]


def near_doc_kernel(place, wh, wl, qh, ql, g0):
    g0[...] = doc_products(wh, wl, qh, ql, 0, BLOCK)


def fold_kernel(place, g0, y1t, y1b, y3t, y3b, d0, d1, d2, d3):
    for k, out in enumerate((d0, d1, d2, d3)):
        half = slice(k % 2 * OWN, (k % 2 + 1) * OWN)
        one, three = (y1t, y3t) if k < 2 else (y1b, y3b)
        out[...] = g0[k * OWN : (k + 1) * OWN, :] + one[half, :] + three[half, :]


def next_over(k, size):
    return (k + 1) % size if k % 2 else (k - 1) % size


def body(query, document, pair_index):
    loop, grp = lax.axis_index("loop"), lax.axis_index("grp")
    c, z = loop & 1, (loop >> 1) & 7
    x, y = grp & 3, (grp >> 2) * 2 + (loop >> 4)
    place = jnp.stack([x, y, z, c]).astype(jnp.int32)
    square = (WIDE, WIDE)
    piece, chip, block = (PIECE, WIDE), (CHIP, WIDE), (BLOCK, WIDE)
    own, totals = (OWN, WIDE), (8, WIDE)

    def one(kernel, shape, *inputs):
        return call(kernel, [(shape, f32)], [place, *inputs])[0]

    with jax.named_scope("gather"):
        d1, d3 = send(document, along_first(-1)), send(document, along_first(1))
        d2 = send(document, along_first(-2))
        u = one(pack_kernel, piece, query, pair_index.astype(f32)[None, :])
        uo = send(u, SWAP)
        a1 = send(u, along_z(-1))
        p1t = jnp.concatenate([document, d1])
        uo, p1t = together((uo, p1t))
        b1 = send(uo, along_z(-1))
        r1t, r3t = send(p1t, along_second(-1)), send(p1t, along_second(1))
        p1b = jnp.concatenate([d2, d3])
        a1, b1, p1b = together((a1, b1, p1b))
        a2 = send(a1, along_z(-1))
        r1b, r3b = send(p1b, along_second(-1)), send(p1b, along_second(1))
        b1, r1t, r3t = together((b1, r1t, r3t))
        b2 = send(b1, along_z(-1))
        r2t = send(r1t, along_second(-1))
        a2, r1b, r3b = together((a2, r1b, r3b))
        a3 = send(a2, along_z(-1))
        r2b = send(r3b, along_second(1))
        b3 = send(b2, along_z(-1))
        s12 = send(one(stack_kernel, (4 * PIECE, WIDE), a1, b1, a2, b2), SWAP)
        a3, r2t = together((a3, r2t))
        a4 = send(a3, along_z(-1))
        b3, r2b = together((b3, r2b))
        s34 = send(one(stack_kernel, (3 * PIECE, WIDE), a3, b3, a4), SWAP)
    tile = [(square, f32)] + [(square, bf16)] * 4 + [(totals, f32)]
    held = call(
        early_kernel,
        tile,
        [place, u, uo, a1, b1, a2, b2, s12, p1t, p1b, r1t, r1b, r3t, r3b],
    )
    st, qh, ql, dh, dl, pair, keep, give = call(
        score_kernel,
        tile + [(totals, f32)] * 2,
        [place, a3, b3, a4, s34, r2t, r2b, *held],
        [pltpu.VMEM((WIDE, 128), f32)],
        aliases=[(7 + k, k) for k in range(6)],
    )
    with jax.named_scope("totals"):
        state = one(merge_kernel, (16, WIDE), keep, send(give, SWAP))
        third_z = (3, 6, 5, 0, 7, 2, 1, 4)
        for move in (
            lambda x, y, z, c: (x, y, z ^ 1, c) if c == 0 else (x ^ 1, y, z, c),
            lambda x, y, z, c: (x, y, next_over(z, 8), c) if c == 0 else (next_over(x, 4), y, z, c),
            lambda x, y, z, c: (x, y, third_z[z], c) if c == 0 else (x, y ^ 1, z, c),
        ):
            state = one(round_kernel, (16, WIDE), state, send(state, permutation(move)))
        last = [
            (source, target)
            for source, target in permutation(lambda x, y, z, c: (x, next_over(y, 4), z, c))
            if source // 8 % 2 == 1
        ]
        mine, give = call(
            last_round_kernel, [(totals, f32)] * 2, [place, state, send(state, last)]
        )
        got = send(give, SWAP)
    wh, wl, a4, a3, b3, first, losses = call(
        weight_kernel,
        [(square, bf16)] * 2 + [(own, f32)] * 3 + [((3 * OWN, WIDE), f32), (totals, f32)],
        [place, st, pair, mine, got, dh, dl],
        [pltpu.VMEM((8, WIDE), f32), pltpu.VMEM((WIDE, 128), f32)],
    )
    with jax.named_scope("scatter"):
        first = send(first, SWAP)
        g1b, g3t, g2t, g2b = call(far_doc_kernel, [(chip, f32)] * 4, [place, wh, wl, qh, ql])
        first, g1b, g3t, g2t, g2b, wh = together((first, g1b, g3t, g2t, g2b, wh))
        a4, b3 = call(first_kernel, [(own, f32)] * 2, [place, a4, b3, first])
        a4, b3, wh = together((a4, b3, wh))
        from1, from3 = send(g2t, along_second(1)), send(g2b, along_second(-1))
        a4, b3 = send(a4, along_z(1)), send(b3, along_z(1))
        y1b, y3t = send(g1b, along_second(1)), send(g3t, along_second(-1))
        a2, b2, a1, b1, near, second = call(
            query_kernel,
            [(own, f32)] * 5 + [((5 * OWN, WIDE), f32)],
            [place, wh, wl, dh, dl],
        )
        a4, b3, from1, from3, second, wh = together((a4, b3, from1, from3, second, wh))
        second = send(second, SWAP)
        a3 = send(one(third_kernel, own, a3, first, a4), along_z(1))
        g1t, g3b = call(
            side_doc_kernel, [(chip, f32)] * 2, [place, wh, wl, qh, ql, from1, from3]
        )
        y1t, y3b = send(g1t, along_second(1)), send(g3b, along_second(-1))
        a2, b2, a1, b1, near = call(
            second_kernel, [(own, f32)] * 5, [place, a2, b2, a1, b1, near, second]
        )
        b2 = send(one(sum_kernel, own, b2, b3), along_z(1))
        g0 = one(near_doc_kernel, block, wh, wl, qh, ql)
        a3, g0 = together((a3, g0))
        a2 = send(one(sum_kernel, own, a2, a3), along_z(1))
        b1 = send(one(sum_kernel, own, b1, b2), along_z(1))
        d0, d1, d2, d3 = call(fold_kernel, [(own, f32)] * 4, [place, g0, y1t, y1b, y3t, y3b])
        d1, d2, d3 = (
            send(d1, along_first(1)),
            send(d2, along_first(2)),
            send(d3, along_first(-1)),
        )
        a1 = send(one(sum_kernel, own, a1, a2), along_z(1))
        grad_doc = d0 + d1 + d2 + d3
        grad_query = near + a1 + send(b1, SWAP)
    row_loss = lax.dynamic_slice(losses[0], (z * CHIP + c * OWN,), (OWN,))
    col_loss = lax.dynamic_slice(losses[1], ((y * 4 + x) * OWN,), (OWN,))
    return row_loss, col_loss, grad_query, grad_doc


def solution(mesh):
    rows, flat_rows = P(AXES, None), P(AXES)
    return jax.shard_map(
        body,
        mesh=mesh,
        in_specs=(rows, rows, flat_rows),
        out_specs=(flat_rows, flat_rows, rows, rows),
        check_vma=False,
    )
```

```python
import functools

import jax
import jax.numpy as jnp
from jax import lax
from jax.experimental import pallas as pl
from jax.experimental.pallas import tpu as pltpu
from jax.sharding import PartitionSpec as P

inv_temp = 20.0
f32, bf16 = jnp.float32, jnp.bfloat16
AXES = ("loop", "grp")
OWN = 64
CHIP = 2 * OWN
PIECE = OWN + 8
WIDE = 1024
BLOCK = 256
EARLY_Q, EARLY_D = 640, 768
VMEM_LIMIT = 12 * 1024 * 1024
GROUPS = ((0, 0), (0, 2), (1, 0), (3, 2), (1, 2), (3, 0), (2, 0), (2, 2))


def flat(x, y, z, c):
    return (((y & 1) * 8 + z) * 2 + c) * 8 + (y >> 1) * 4 + x


def permutation(move):
    return [
        (flat(x, y, z, c), flat(*move(x, y, z, c)))
        for x in range(4)
        for y in range(4)
        for z in range(8)
        for c in range(2)
    ]


def along_first(delta):
    return permutation(
        lambda x, y, z, c: ((x + delta) % 4, y, z, c) if c == 0 else (x, (y + delta) % 4, z, c)
    )


def along_second(delta):
    return permutation(
        lambda x, y, z, c: (x, (y + delta) % 4, z, c) if c == 0 else ((x + delta) % 4, y, z, c)
    )


def along_z(delta):
    return permutation(
        lambda x, y, z, c: (x, y, (z + delta) % 8, c) if c == 0 else (x, y, (z - delta) % 8, c)
    )


SWAP = permutation(lambda x, y, z, c: (x, y, z, 1 - c))


def send(value, perm):
    return lax.ppermute(value, AXES, perm)


together = lax.optimization_barrier


def split(value):
    high = value.astype(bf16)
    return high, (value - high.astype(f32)).astype(bf16)


def dot3(ah, al, bh, bl, dims):
    dot = functools.partial(
        lax.dot_general, dimension_numbers=(dims, ((), ())), preferred_element_type=f32
    )
    return dot(ah, bh) + dot(ah, bl) + dot(al, bh)


def call(kernel, shapes, inputs, scratch=(), aliases=()):
    held = [pltpu.with_memory_space_constraint(a, pltpu.VMEM) for a in inputs[1:]]
    return pl.pallas_call(
        kernel,
        out_shape=[pltpu.VMEM(s, t) for s, t in shapes],
        in_specs=[pl.BlockSpec(memory_space=pltpu.SMEM)]
        + [pl.BlockSpec(memory_space=pltpu.VMEM)] * len(held),
        out_specs=[pl.BlockSpec(memory_space=pltpu.VMEM)] * len(shapes),
        scratch_shapes=list(scratch),
        input_output_aliases=dict(aliases),
        compiler_params=pltpu.CompilerParams(vmem_limit_bytes=VMEM_LIMIT),
    )(inputs[0], *held)


def block_z(z, c, block):
    sign = 1 - 2 * c
    steps = (0, 1, -1, 2, -2, 3, -3, 4)[block]
    return (z + sign * steps) & 7


def doc_chip(x, y, c, first, second):
    dx = jnp.where(c == 0, first, second)
    dy = jnp.where(c == 0, second, first)
    return ((y + dy) & 3) * 4 + ((x + dx) & 3)


def doc_piece(x, y, c, piece):
    second, first = GROUPS[piece // 2]
    return doc_chip(x, y, c, first + piece % 2, second)


def doc_ids(block, x, y, z, c):
    row = lax.broadcasted_iota(jnp.int32, (OWN, 1), 0)
    ids = []
    for piece in range(block * 4, block * 4 + 4):
        chip = doc_piece(x, y, c, piece)
        ids.append(row + flat(chip & 3, chip >> 2, z, c) * OWN)
    return jnp.concatenate(ids, axis=0).astype(f32)


def put(high, low, ref, start, count, row):
    h, l = split(ref[start : start + count, :])
    high[row : row + count, :] = h
    low[row : row + count, :] = l


def pack_kernel(place, query, pairs, out):
    out[0:OWN, :] = query[...]
    out[OWN:, :] = jnp.zeros((8, WIDE), f32)
    out[OWN : OWN + 1, :OWN] = pairs[...]


def stack_kernel(place, *refs):
    for k, ref in enumerate(refs[:-1]):
        refs[-1][k * PIECE : (k + 1) * PIECE, :] = ref[...]


def put_queries(qh, ql, pair, block, mine, mine_at, other, other_at):
    put(qh, ql, mine, mine_at, OWN, block * CHIP)
    put(qh, ql, other, other_at, OWN, block * CHIP + OWN)
    first = mine[mine_at + OWN : mine_at + PIECE, :CHIP]
    last = other[other_at + OWN : other_at + PIECE, :CHIP]
    pair[:, block * CHIP : (block + 1) * CHIP] = first + pltpu.roll(last, OWN, 1)


def early_kernel(place, u, uo, a1, b1, a2, b2, s12, p1t, p1b, r1t, r1b, r3t, r3b, *outs):
    st, qh, ql, dh, dl, pair = outs
    put_queries(qh, ql, pair, 0, u, 0, uo, 0)
    put_queries(qh, ql, pair, 1, a1, 0, b1, 0)
    put_queries(qh, ql, pair, 2, s12, PIECE, s12, 0)
    put_queries(qh, ql, pair, 3, a2, 0, b2, 0)
    put_queries(qh, ql, pair, 4, s12, 3 * PIECE, s12, 2 * PIECE)
    for k, ref in enumerate((p1t, p1b, r1t, r3b, r1b, r3t)):
        put(dh, dl, ref, 0, CHIP, k * CHIP)
    q = slice(0, EARLY_Q)
    for b in range(3):
        at = slice(b * BLOCK, (b + 1) * BLOCK)
        s = dot3(dh[at, :], dl[at, :], qh[q, :], ql[q, :], ((1,), (1,)))
        st[at, q] = s * inv_temp


def score_kernel(place, a3, b3, a4, s34, r2t, r2b, *refs):
    st, qh, ql, dh, dl, pair, keep, give, mixed = refs[6:]
    x, y, z, c = place[0], place[1], place[2], place[3]
    put_queries(qh, ql, pair, 5, a3, 0, b3, 0)
    put_queries(qh, ql, pair, 6, s34, PIECE, s34, 0)
    put_queries(qh, ql, pair, 7, a4, 0, s34, 2 * PIECE)
    put(dh, dl, r2t, 0, CHIP, EARLY_D)
    put(dh, dl, r2b, 0, CHIP, EARLY_D + CHIP)
    pairs = pair[0:1, :]
    lane = lax.broadcasted_iota(jnp.int32, (BLOCK, 128), 1)
    for b in range(4):
        at = slice(b * BLOCK, (b + 1) * BLOCK)
        q = slice(EARLY_Q if b < 3 else 0, WIDE)
        s = dot3(dh[at, :], dl[at, :], qh[q, :], ql[q, :], ((1,), (1,)))
        st[at, q] = s * inv_temp
        s = st[at, :]
        picked = jnp.where(pairs == doc_ids(b, x, y, z, c), s, 0.0)
        cm = jnp.max(s, axis=1, keepdims=True)
        ce = jnp.sum(jnp.exp(s - cm), axis=1, keepdims=True)
        cp = jnp.sum(picked, axis=1, keepdims=True)
        stats = jnp.where(lane == 0, cm, jnp.where(lane == 1, ce, cp))
        for a in range(4):
            row = pl.multiple_of(doc_piece(x, y, c, b * 4 + a) * OWN, OWN)
            mixed[pl.ds(row, OWN), :] = stats[a * OWN : (a + 1) * OWN, :]
        bm = jnp.max(s, axis=0, keepdims=True)
        bp = jnp.sum(picked, axis=0, keepdims=True)
        if b == 0:
            rm, rp = bm, bp
            re = jnp.sum(jnp.exp(s - rm), axis=0, keepdims=True)
        else:
            top = jnp.maximum(rm, bm)
            re = re * jnp.exp(rm - top) + jnp.sum(jnp.exp(s - top), axis=0, keepdims=True)
            rm, rp = top, rp + bp
    rows = jnp.concatenate([rm, re, rp, jnp.zeros((5, WIDE), f32)], axis=0)

    def put_stats(row_out, col_out):
        for block in range(8):
            part = rows[:, block * CHIP : (block + 1) * CHIP]
            part = jnp.where(c == 0, part, pltpu.roll(part, OWN, 1))
            at = pl.multiple_of(block_z(z, c, block) * CHIP, CHIP)
            row_out[:, pl.ds(at, CHIP)] = part
        for b in range(4):
            at = slice(b * BLOCK, (b + 1) * BLOCK)
            col_out[:, at] = mixed[at, :].T[0:8, :]

    @pl.when(c == 0)
    def _():
        put_stats(keep, give)

    @pl.when(c == 1)
    def _():
        put_stats(give, keep)


def combine(a, b):
    top = jnp.maximum(a[0:1, :], b[0:1, :])
    total = a[1:2, :] * jnp.exp(a[0:1, :] - top) + b[1:2, :] * jnp.exp(b[0:1, :] - top)
    return jnp.concatenate(
        [top, total, a[2:3, :] + b[2:3, :], jnp.zeros((5, WIDE), f32)], axis=0
    )


def merge_kernel(place, keep, got, state):
    mine, theirs = keep[...], got[...]
    both = combine(mine, theirs)
    state[0:8, :] = jnp.where(place[3] == 0, both, mine)
    state[8:16, :] = jnp.where(place[3] == 0, both, theirs)


def round_kernel(place, state, got, out):
    out[0:8, :] = combine(state[0:8, :], got[0:8, :])
    out[8:16, :] = combine(state[8:16, :], got[8:16, :])


def last_round_kernel(place, state, got, mine, give):
    for out, at in ((mine, slice(0, 8)), (give, slice(8, 16))):
        so_far = state[at, :]
        out[...] = jnp.where(place[3] == 0, so_far, combine(so_far, got[at, :]))


def sum_kernel(place, *refs):
    *parts, out = refs
    out[...] = sum((part[...] for part in parts[1:]), parts[0][...])


def query_products(wh, wl, dh, dl, lo, hi):
    return dot3(wh[:, lo:hi], wl[:, lo:hi], dh[...], dl[...], ((0,), (0,)))


def weight_kernel(place, st, pair, mine, got, dh, dl, *refs):
    wh, wl, a4, a3, b3, first, losses, lse, columns = refs
    x, y, z, c = place[0], place[1], place[2], place[3]
    row_stats = jnp.where(c == 0, mine[...], got[...])
    col_stats = jnp.where(c == 0, got[...], mine[...])
    row_lse = row_stats[0:1, :] + jnp.log(row_stats[1:2, :])
    col_lse = col_stats[0:1, :] + jnp.log(col_stats[1:2, :])
    losses[...] = jnp.concatenate(
        [row_lse - row_stats[2:3, :], col_lse - col_stats[2:3, :], jnp.zeros((6, WIDE), f32)],
        axis=0,
    )
    lse[...] = jnp.broadcast_to(row_lse, (8, WIDE))
    parts = []
    for block in range(8):
        at = pl.multiple_of(block_z(z, c, block) * CHIP, CHIP)
        part = lse[:, pl.ds(at, CHIP)]
        parts.append(jnp.where(c == 0, part, pltpu.roll(part, OWN, 1)))
    row_lse = jnp.concatenate(parts, axis=1)[0:1, :]
    for b in range(4):
        at = slice(b * BLOCK, (b + 1) * BLOCK)
        columns[at, :] = jnp.broadcast_to(col_lse[:, at], (128, BLOCK)).T
    pairs = pair[0:1, :]
    for b in range(4):
        at = slice(b * BLOCK, (b + 1) * BLOCK)
        s = st[at, :]
        parts = []
        for a in range(4):
            row = pl.multiple_of(doc_piece(x, y, c, b * 4 + a) * OWN, OWN)
            parts.append(columns[pl.ds(row, OWN), :])
        cl = jnp.concatenate(parts, axis=0)[:, 0:1]
        w = (jnp.exp(s - row_lse) + jnp.exp(s - cl)) * (0.5 * inv_temp)
        w = w - jnp.where(pairs == doc_ids(b, x, y, z, c), inv_temp, 0.0)
        h, l = split(w)
        wh[at, :] = h
        wl[at, :] = l
    g = query_products(wh, wl, dh, dl, EARLY_Q, WIDE)
    a3[...] = g[:OWN]
    b3[...] = g[OWN:CHIP]
    a4[...] = g[2 * CHIP : 2 * CHIP + OWN]
    first[0:OWN, :] = g[2 * CHIP + OWN :]
    first[OWN : 2 * OWN, :] = g[CHIP + OWN : 2 * CHIP]
    first[2 * OWN :, :] = g[CHIP : CHIP + OWN]


def first_kernel(place, a4, b3, first, a4_out, b3_out):
    a4_out[...] = a4[...] + first[0:OWN, :]
    b3_out[...] = b3[...] + first[2 * OWN :, :]


def third_kernel(place, a3, first, from4, out):
    out[...] = a3[...] + first[OWN : 2 * OWN, :] + from4[...]


def query_kernel(place, wh, wl, dh, dl, a2, b2, a1, b1, near, second):
    g = query_products(wh, wl, dh, dl, 0, EARLY_Q)
    near[...] = g[:OWN]
    a1[...] = g[CHIP : CHIP + OWN]
    b1[...] = g[CHIP + OWN : 2 * CHIP]
    a2[...] = g[3 * CHIP : 3 * CHIP + OWN]
    b2[...] = g[3 * CHIP + OWN : 4 * CHIP]
    second[0:OWN, :] = g[4 * CHIP + OWN :]
    second[OWN : 2 * OWN, :] = g[4 * CHIP : 4 * CHIP + OWN]
    second[2 * OWN : 3 * OWN, :] = g[2 * CHIP + OWN : 3 * CHIP]
    second[3 * OWN : 4 * OWN, :] = g[2 * CHIP : 2 * CHIP + OWN]
    second[4 * OWN :, :] = g[OWN:CHIP]


def second_kernel(place, a2, b2, a1, b1, near, second, a2_out, b2_out, a1_out, b1_out, near_out):
    pairs = ((a2, a2_out), (b2, b2_out), (a1, a1_out), (b1, b1_out), (near, near_out))
    for k, (part, out) in enumerate(pairs):
        out[...] = part[...] + second[k * OWN : (k + 1) * OWN, :]


def doc_products(wh, wl, qh, ql, lo, hi):
    return dot3(wh[lo:hi, :], wl[lo:hi, :], qh[...], ql[...], ((1,), (0,)))


def far_doc_kernel(place, wh, wl, qh, ql, g1b, g3t, g2t, g2b):
    g = doc_products(wh, wl, qh, ql, 2 * BLOCK, WIDE)
    for k, out in enumerate((g1b, g3t, g2t, g2b)):
        out[...] = g[k * CHIP : (k + 1) * CHIP]


def side_doc_kernel(place, wh, wl, qh, ql, from1, from3, g1t, g3b):
    g = doc_products(wh, wl, qh, ql, BLOCK, 2 * BLOCK)
    g1t[...] = g[:CHIP] + from1[...]
    g3b[...] = g[CHIP:] + from3[...]


def near_doc_kernel(place, wh, wl, qh, ql, g0):
    g0[...] = doc_products(wh, wl, qh, ql, 0, BLOCK)


def fold_kernel(place, g0, y1t, y1b, y3t, y3b, d0, d1, d2, d3):
    for k, out in enumerate((d0, d1, d2, d3)):
        half = slice(k % 2 * OWN, (k % 2 + 1) * OWN)
        one, three = (y1t, y3t) if k < 2 else (y1b, y3b)
        out[...] = g0[k * OWN : (k + 1) * OWN, :] + one[half, :] + three[half, :]


def next_over(k, size):
    return (k + 1) % size if k % 2 else (k - 1) % size


def body(query, document, pair_index):
    loop, grp = lax.axis_index("loop"), lax.axis_index("grp")
    c, z = loop & 1, (loop >> 1) & 7
    x, y = grp & 3, (grp >> 2) * 2 + (loop >> 4)
    place = jnp.stack([x, y, z, c]).astype(jnp.int32)
    square = (WIDE, WIDE)
    piece, chip, block = (PIECE, WIDE), (CHIP, WIDE), (BLOCK, WIDE)
    own, totals = (OWN, WIDE), (8, WIDE)

    def one(kernel, shape, *inputs):
        return call(kernel, [(shape, f32)], [place, *inputs])[0]

    with jax.named_scope("gather"):
        d1, d3 = send(document, along_first(-1)), send(document, along_first(1))
        d2 = send(document, along_first(-2))
        u = one(pack_kernel, piece, query, pair_index.astype(f32)[None, :])
        uo = send(u, SWAP)
        a1 = send(u, along_z(-1))
        p1t = jnp.concatenate([document, d1])
        uo, p1t = together((uo, p1t))
        b1 = send(uo, along_z(-1))
        r1t, r3t = send(p1t, along_second(-1)), send(p1t, along_second(1))
        p1b = jnp.concatenate([d2, d3])
        a1, p1b = together((a1, p1b))
        a2 = send(a1, along_z(-1))
        r1b, r3b = send(p1b, along_second(-1)), send(p1b, along_second(1))
        b1, r1t = together((b1, r1t))
        b2 = send(b1, along_z(-1))
        r2t = send(r1t, along_second(-1))
        a2, r1b, r3b = together((a2, r1b, r3b))
        a3 = send(a2, along_z(-1))
        r2b = send(r3b, along_second(1))
        b3 = send(b2, along_z(-1))
        s12 = send(one(stack_kernel, (4 * PIECE, WIDE), a1, b1, a2, b2), SWAP)
        a3, r2t = together((a3, r2t))
        a4 = send(a3, along_z(-1))
        b3, r2b = together((b3, r2b))
        s34 = send(one(stack_kernel, (3 * PIECE, WIDE), a3, b3, a4), SWAP)
    tile = [(square, f32)] + [(square, bf16)] * 4 + [(totals, f32)]
    held = call(
        early_kernel,
        tile,
        [place, u, uo, a1, b1, a2, b2, s12, p1t, p1b, r1t, r1b, r3t, r3b],
    )
    st, qh, ql, dh, dl, pair, keep, give = call(
        score_kernel,
        tile + [(totals, f32)] * 2,
        [place, a3, b3, a4, s34, r2t, r2b, *held],
        [pltpu.VMEM((WIDE, 128), f32)],
        aliases=[(7 + k, k) for k in range(6)],
    )
    with jax.named_scope("totals"):
        state = one(merge_kernel, (16, WIDE), keep, send(give, SWAP))
        third_z = (3, 6, 5, 0, 7, 2, 1, 4)
        for move in (
            lambda x, y, z, c: (x, y, z ^ 1, c) if c == 0 else (x ^ 1, y, z, c),
            lambda x, y, z, c: (x, y, next_over(z, 8), c) if c == 0 else (next_over(x, 4), y, z, c),
            lambda x, y, z, c: (x, y, third_z[z], c) if c == 0 else (x, y ^ 1, z, c),
        ):
            state = one(round_kernel, (16, WIDE), state, send(state, permutation(move)))
        last = [
            (source, target)
            for source, target in permutation(lambda x, y, z, c: (x, next_over(y, 4), z, c))
            if source // 8 % 2 == 1
        ]
        mine, give = call(
            last_round_kernel, [(totals, f32)] * 2, [place, state, send(state, last)]
        )
        got = send(give, SWAP)
    wh, wl, a4, a3, b3, first, losses = call(
        weight_kernel,
        [(square, bf16)] * 2 + [(own, f32)] * 3 + [((3 * OWN, WIDE), f32), (totals, f32)],
        [place, st, pair, mine, got, dh, dl],
        [pltpu.VMEM((8, WIDE), f32), pltpu.VMEM((WIDE, 128), f32)],
    )
    with jax.named_scope("scatter"):
        first = send(first, SWAP)
        g1b, g3t, g2t, g2b = call(far_doc_kernel, [(chip, f32)] * 4, [place, wh, wl, qh, ql])
        first, g1b, g3t, g2t, g2b, wh = together((first, g1b, g3t, g2t, g2b, wh))
        a4, b3 = call(first_kernel, [(own, f32)] * 2, [place, a4, b3, first])
        a4, b3, wh = together((a4, b3, wh))
        from1, from3 = send(g2t, along_second(1)), send(g2b, along_second(-1))
        a4, b3 = send(a4, along_z(1)), send(b3, along_z(1))
        y1b, y3t = send(g1b, along_second(1)), send(g3t, along_second(-1))
        a2, b2, a1, b1, near, second = call(
            query_kernel,
            [(own, f32)] * 5 + [((5 * OWN, WIDE), f32)],
            [place, wh, wl, dh, dl],
        )
        a4, b3, from1, from3, second, wh = together((a4, b3, from1, from3, second, wh))
        second = send(second, SWAP)
        a3 = send(one(third_kernel, own, a3, first, a4), along_z(1))
        g1t, g3b = call(
            side_doc_kernel, [(chip, f32)] * 2, [place, wh, wl, qh, ql, from1, from3]
        )
        y1t, y3b = send(g1t, along_second(1)), send(g3b, along_second(-1))
        a2, b2, a1, b1, near = call(
            second_kernel, [(own, f32)] * 5, [place, a2, b2, a1, b1, near, second]
        )
        b2 = send(one(sum_kernel, own, b2, b3), along_z(1))
        g0 = one(near_doc_kernel, block, wh, wl, qh, ql)
        a3, g0 = together((a3, g0))
        a2 = send(one(sum_kernel, own, a2, a3), along_z(1))
        b1 = send(one(sum_kernel, own, b1, b2), along_z(1))
        d0, d1, d2, d3 = call(fold_kernel, [(own, f32)] * 4, [place, g0, y1t, y1b, y3t, y3b])
        d1, d2, d3 = (
            send(d1, along_first(1)),
            send(d2, along_first(2)),
            send(d3, along_first(-1)),
        )
        a1 = send(one(sum_kernel, own, a1, a2), along_z(1))
        grad_doc = d0 + d1 + d2 + d3
        grad_query = near + a1 + send(b1, SWAP)
    row_loss = lax.dynamic_slice(losses[0], (z * CHIP + c * OWN,), (OWN,))
    col_loss = lax.dynamic_slice(losses[1], ((y * 4 + x) * OWN,), (OWN,))
    return row_loss, col_loss, grad_query, grad_doc


def solution(mesh):
    rows, flat_rows = P(AXES, None), P(AXES)
    return jax.shard_map(
        body,
        mesh=mesh,
        in_specs=(rows, rows, flat_rows),
        out_specs=(flat_rows, flat_rows, rows, rows),
        check_vma=False,
    )
```
